1024 devices in a mesh: dp: 64 (over y_lo, z), mp: 16 (over y_hi, x, core).
Axes of the slice: x: 4, y: 4 (y_hi: 2, y_lo: 2; y = y_hi * 2 + y_lo), z: 32, core: 2. Of those that a mesh axis runs over, the one named last changes fastest.
Arguments:
- bag_ids: int32 [4096, 64, 16], P('dp'), may hold values from 0 to 1023
- tables: bfloat16 [64, 1024, 256], P(None, 'mp'), may hold values from -1.5 to 1.5
- down_proj: bfloat16 [16384, 256], P('mp'), may hold values from -0.046875 to 0.046875
- up_proj: bfloat16 [256, 16384], P(None, 'mp'), may hold values from -0.375 to 0.375
- cotangent: bfloat16 [4096, 16384], P('dp', 'mp'), may hold values from -6 to 6
Outputs:
- cross_out: bfloat16 [4096, 16384], P('dp', 'mp')
- table_grads: bfloat16 [64, 64, 1024, 256], P('dp', None, 'mp')
- down_grad: float32 [16384, 256], P('mp')
- up_grad: float32 [256, 16384], P(None, 'mp')
The draws below stay inside these ranges and needn't reach their ends.
All inputs are finite; a program needn't handle non-finite values.
Results may differ from the reference program's by a relative error of at most 0.028.
Values may be sent and summed in bfloat16 or wider, within the bound.
No kernel may reach another device: no remote copies, remote signals or barrier semaphores. Data moves between devices by JAX's collectives and lax.ppermute only.
A program may use at most 64 MiB of HBM per device.

```python
import math
import jax
import jax.numpy as jnp
import numpy as np
from jax import lax

E = 256
F = 64
R = 256
L = 16
B_GRP = 64
ROWS_DEV = 64
ROWS = 1024
BATCH = 4096
D_IN = 16384
N_DP = 64
N_MP = 16


def touch_ends(array, rng, least, largest):
    index_at = [jax.random.randint(jax.random.fold_in(rng, axis), (), 0, length) for axis, length in enumerate(array.shape)]
    widest = array.shape.index(max(array.shape))
    beside = index_at[:widest] + [(index_at[widest] + 1) % array.shape[widest]] + index_at[widest + 1:]
    return array.at[tuple(index_at)].set(least).at[tuple(beside)].set(largest)


def steps_of(key, extent, cuts, least, largest):
    def one(position, shards_of):
        draws = jax.random.uniform(jax.random.fold_in(jax.random.fold_in(key, 6), position), (shards_of,), jnp.float32, least / len(cuts), largest / len(cuts))
        return jnp.repeat(jnp.exp(draws), extent[position] // shards_of).reshape((-1,) + (1,) * (len(extent) - position - 1))

    factor_of = one(*cuts[0])
    for cut in cuts[1:]:
        factor_of = factor_of * one(*cut)
    return factor_of


def cumulative_ranks(count, skew):
    weights = [(1 << 20) // math.isqrt(rank ** skew) + 1 for rank in range(1, count + 1)]
    deviation = 1 + sum(weights) // (1 << 30)
    return np.cumsum(np.array([max(1, weight // deviation) for weight in weights]))


def ranked(rng, shape, count, skew):
    listing = cumulative_ranks(count, skew)
    ticket = jax.random.randint(jax.random.fold_in(rng, 1), shape, 0, int(listing[count - 1]))
    standing = jnp.searchsorted(jnp.asarray(listing, jnp.int32), ticket, side="right")
    return jax.random.permutation(jax.random.fold_in(rng, 2), count)[standing].astype(jnp.int32)


def scatter_about(stream_key, shape, width, bound, split=(), held_as=jnp.bfloat16):
    values = width * jax.random.normal(stream_key, shape, jnp.float32)
    if split:
        values = values * steps_of(stream_key, shape, split, -0.22, 0.18)
    return jnp.clip(values, -bound, bound).astype(held_as)


def setup_inputs(seed: int = 0) -> dict:
    splits = jax.random.split(jax.random.key(seed), 6)
    bag_ids = touch_ends(ranked(splits[0], (BATCH, F, L), ROWS, 2), jax.random.fold_in(splits[0], 3), 0, ROWS - 1).astype(jnp.int32)
    tables = scatter_about(splits[1], (F, ROWS, E), 0.25, 1.5, ((1, 16),))
    down_proj = scatter_about(splits[2], (D_IN, R), D_IN ** -0.5, 0.046875, ((0, 16),))
    up_proj = scatter_about(splits[3], (R, D_IN), R ** -0.5, 0.375, ((1, 16),))
    cotangent = scatter_about(splits[4], (BATCH, D_IN), 1.0, 6.0, ((0, 64), (1, 16)))
    return dict(bag_ids=bag_ids, tables=tables, down_proj=down_proj, up_proj=up_proj, cotangent=cotangent)


def reference(bag_ids, tables, down_proj, up_proj, cotangent):
    grouped_ids = bag_ids.reshape(N_DP, B_GRP, F, L)
    grouped_grad = cotangent.reshape(N_DP, B_GRP, D_IN)
    feature_axis = jnp.arange(F, dtype=jnp.int32)[None, :, None]
    sample_axis = jnp.arange(B_GRP, dtype=jnp.int32)[:, None, None]

    def group_step(carry, inputs):
        group_ids, group_grad = inputs
        looked_up = tables[feature_axis, group_ids].astype(jnp.float32)
        owner_shard = (group_ids // ROWS_DEV).astype(jnp.int32)
        partial_value = jnp.zeros((N_MP, B_GRP, F, E), jnp.float32).at[owner_shard, sample_axis, feature_axis].add(looked_up)
        partial_value = partial_value.astype(jnp.bfloat16)
        pooled = jnp.sum(partial_value.astype(jnp.float32), axis=0).astype(jnp.bfloat16).reshape(B_GRP, D_IN)
        rank_act = jnp.dot(pooled, down_proj, preferred_element_type=jnp.float32).astype(jnp.bfloat16)
        scale_map = jnp.dot(rank_act, up_proj, preferred_element_type=jnp.float32)
        pooled_f = pooled.astype(jnp.float32)
        cross_out = (pooled_f * scale_map + pooled_f).astype(jnp.bfloat16)
        upstream = group_grad.astype(jnp.float32)
        scale_grad = (upstream * pooled_f).astype(jnp.bfloat16)
        up_part = jnp.dot(rank_act.T, scale_grad, preferred_element_type=jnp.float32)
        rank_grad = jnp.dot(scale_grad, up_proj.T, preferred_element_type=jnp.float32).astype(jnp.bfloat16)
        down_part = jnp.dot(pooled.T, rank_grad, preferred_element_type=jnp.float32)
        back = jnp.dot(rank_grad, down_proj.T, preferred_element_type=jnp.float32)
        pooled_grad = (upstream * scale_map + upstream + back).astype(jnp.bfloat16)
        spread = jnp.broadcast_to(pooled_grad.reshape(B_GRP, F, 1, E).astype(jnp.float32), (B_GRP, F, L, E))
        table_grad = jnp.zeros((F, ROWS, E), jnp.float32).at[feature_axis, group_ids].add(spread).astype(jnp.bfloat16)
        return (carry[0] + down_part, carry[1] + up_part), (cross_out, table_grad)

    start = (jnp.zeros((D_IN, R), jnp.float32), jnp.zeros((R, D_IN), jnp.float32))
    (down_grad, up_grad), (cross_out, table_grads) = lax.scan(group_step, start, (grouped_ids, grouped_grad))
    return cross_out.reshape(BATCH, D_IN), table_grads, down_grad, up_grad
```

```python
import jax
import jax.numpy as jnp
from jax import lax
from jax.experimental import pallas as pl
from jax.experimental.pallas import tpu as pltpu
from jax.sharding import PartitionSpec as P

BF16 = jnp.bfloat16
F32 = jnp.float32
VMEM_LIMIT = 48 * 1024 * 1024

QUAD = 4


def layout_of(dp_count, mp_count):
    depth = dp_count // 2
    pairs = depth // 2

    def member(pair, quad):
        return (quad // 2) * depth + pair * 2 + quad % 2

    quads = [[member(pair, quad) for quad in range(QUAD)] for pair in range(pairs)]
    lines = [[member(pair, quad) for pair in range(pairs)] for quad in range(QUAD)]
    blocks = [
        [member(pair, quad) * mp_count + index for index in range(mp_count) for quad in range(QUAD)]
        for pair in range(pairs)
    ]
    return quads, lines, blocks


def call(body, out_shape, *operands):
    return pl.pallas_call(
        body,
        out_shape=out_shape,
        compiler_params=pltpu.CompilerParams(vmem_limit_bytes=VMEM_LIMIT),
    )(*operands)


def contract(left, right, left_dim, right_dim):
    return lax.dot_general(
        left, right, (((left_dim,), (right_dim,)), ((), ())), preferred_element_type=F32
    )


def count_body(ids_ref, counts_ref):
    bag_size, columns = ids_ref.shape
    step = 64

    def rows_at(index, carry):
        base = pl.multiple_of(index * step, step)
        rows = lax.broadcasted_iota(jnp.int32, (step, columns), 0) + base
        total = jnp.zeros((step, columns), F32)
        for slot in range(bag_size):
            total = total + jnp.where(rows == ids_ref[slot : slot + 1, :], 1.0, 0.0)
        counts_ref[pl.ds(base, step), :] = total.astype(BF16)
        return carry

    lax.fori_loop(0, counts_ref.shape[0] // step, rows_at, 0)


def forward_body(counts_ref, table_ref, grad_ref, down_ref, up_ref, pooled_ref, scaled_ref, part_ref):
    samples = grad_ref.shape[0]
    pooled = contract(counts_ref[...], table_ref[...], 0, 0).astype(BF16)
    pooled_ref[...] = pooled
    scaled = (grad_ref[...].astype(F32) * pooled.astype(F32)).astype(BF16)
    scaled_ref[...] = scaled
    part_ref[:samples, :] = contract(pooled, down_ref[...], 1, 0).astype(BF16)
    part_ref[samples:, :] = contract(scaled, up_ref[...], 1, 1).astype(BF16)


def cross_body(ranks_ref, pooled_ref, scaled_ref, grad_ref, down_ref, up_ref, parts_ref, back_ref):
    samples = grad_ref.shape[0]
    rank_act = ranks_ref[:samples, :]
    rank_grad = ranks_ref[samples:, :]
    pooled = pooled_ref[...]
    parts_ref[0] = contract(rank_act, scaled_ref[...], 0, 0).astype(BF16)
    parts_ref[1] = contract(pooled, rank_grad, 0, 0).astype(BF16)
    scale_map = contract(rank_act, up_ref[...], 1, 0)
    pooled_f = pooled.astype(F32)
    cross = (pooled_f * scale_map + pooled_f).astype(BF16)
    upstream = grad_ref[...].astype(F32)
    back = contract(rank_grad, down_ref[...], 1, 1)
    pooled_grad = (upstream * scale_map + upstream + back).astype(BF16)
    group = samples // QUAD
    for quad in range(QUAD):
        back_ref[quad, 0] = cross[quad * group : (quad + 1) * group]
        back_ref[quad, 1] = pooled_grad[quad * group : (quad + 1) * group]


def table_body(counts_ref, back_ref, cross_ref, grads_ref):
    ways, _, rows, embed = grads_ref.shape
    group = back_ref.shape[2]
    blocks = []
    for quad in range(QUAD):
        cross_ref[:, quad * embed : (quad + 1) * embed] = back_ref[quad, 0]
        blocks.append(back_ref[quad, 1])
    zero = jnp.zeros((group, embed), BF16)
    spread = jnp.concatenate(
        [
            jnp.concatenate([blocks[quad] if quad == other else zero for other in range(QUAD)], axis=1)
            for quad in range(QUAD)
        ],
        axis=0,
    )
    step = 4 * rows

    def rows_at(index, carry):
        base = pl.multiple_of(index * step, step)
        grads = contract(counts_ref[pl.ds(base, step), :], spread, 1, 0).astype(BF16)
        for part in range(4):
            for quad in range(QUAD):
                grads_ref[index * 4 + part, quad] = grads[
                    part * rows : (part + 1) * rows, quad * embed : (quad + 1) * embed
                ]
        return carry

    lax.fori_loop(0, ways // 4, rows_at, 0)


def weights_body(sums_ref, down_ref, up_ref):
    width = sums_ref.shape[3]
    for quad in range(QUAD):
        up_ref[:, quad * width : (quad + 1) * width] = sums_ref[quad, 0].astype(F32)
        down_ref[quad * width : (quad + 1) * width, :] = sums_ref[quad, 1].astype(F32)


def shape_of(shape, dtype=BF16):
    return jax.ShapeDtypeStruct(shape, dtype)


def shards(bag_ids, tables, down_proj, up_proj, cotangent):
    dp_count, ways = lax.axis_size("dp"), lax.axis_size("mp")
    quads, lines, blocks = layout_of(dp_count, ways)
    place = lax.axis_index("dp")
    quad = (place // (dp_count // 2)) * 2 + place % 2
    shard_index = lax.axis_index("mp")
    group, feature_count, bag_size = bag_ids.shape
    _, rows, embed = tables.shape
    rank = down_proj.shape[1]
    samples = QUAD * group

    def exchange(value, axis, groups=None):
        return lax.all_to_all(value, axis, 0, 0, axis_index_groups=groups, tiled=True)

    def spread_over(value, count):
        return jnp.broadcast_to(value[None], (count,) + value.shape)

    with jax.named_scope("inputs"):
        own_ids = lax.dynamic_slice_in_dim(bag_ids, shard_index * QUAD, QUAD, 1)
        own_ids = jnp.transpose(own_ids, (1, 2, 0))
        table_parts = lax.dynamic_index_in_dim(
            tables.reshape(ways, QUAD, rows, embed), quad, 1, keepdims=False
        )
        grad_parts = jnp.transpose(cotangent.reshape(group, QUAD, embed), (1, 0, 2))
        quad_ids = exchange(own_ids, "dp", quads)
        table = exchange(table_parts, "mp").reshape(ways * rows, embed)
        quad_grad = exchange(grad_parts, "dp", quads).reshape(samples, embed)
        down = lax.dynamic_slice_in_dim(down_proj, quad * embed, embed, 0)
        up = lax.dynamic_slice_in_dim(up_proj, quad * embed, embed, 1)

    def count(ids):
        columns = jnp.transpose(ids, (1, 0, 2)).reshape(bag_size, samples)
        return call(count_body, shape_of((ways * rows, samples)), columns)

    with jax.named_scope("counts"):
        quad_counts = count(quad_ids)
        own_counts = count(own_ids)

    with jax.named_scope("forward"):
        pooled, scaled, part = call(
            forward_body,
            (shape_of((samples, embed)), shape_of((samples, embed)), shape_of((2 * samples, rank))),
            quad_counts, table, quad_grad, down, up,
        )
    with jax.named_scope("ranks"):
        members = QUAD * ways
        pieces = exchange(part.reshape(members, 2 * samples // members, rank), ("dp", "mp"), blocks)
        piece = jnp.sum(pieces.astype(F32), axis=0).astype(BF16)
        ranks = exchange(spread_over(piece, members), ("dp", "mp"), blocks).reshape(2 * samples, rank)

    with jax.named_scope("cross"):
        parts, back = call(
            cross_body,
            (shape_of((2, embed, rank)), shape_of((QUAD, 2, group, embed))),
            ranks, pooled, scaled, quad_grad, down, up,
        )
    with jax.named_scope("weights"):
        pairs = dp_count // QUAD
        slices = exchange(parts.reshape(pairs, 2 * embed // pairs, rank), "dp", lines)
        own_slice = jnp.sum(slices.astype(F32), axis=0).astype(BF16)
        sums = exchange(spread_over(own_slice, pairs), "dp", lines).reshape(2, embed, rank)
        every = exchange(spread_over(sums, QUAD), "dp", quads)
        down_grad, up_grad = call(
            weights_body, (shape_of(down_proj.shape, F32), shape_of(up_proj.shape, F32)), every
        )
    with jax.named_scope("tables"):
        own_back = exchange(back, "dp", quads)
        cross_out, grads = call(
            table_body,
            (shape_of((group, QUAD * embed)), shape_of((ways, QUAD, rows, embed))),
            own_counts, own_back,
        )
        table_grads = exchange(grads, "mp").reshape(1, feature_count, rows, embed)
    return (cross_out, table_grads, down_grad, up_grad)


def solution(mesh):
    placed = (P("dp", None, None), P(None, "mp", None), P("mp", None), P(None, "mp"), P("dp", "mp"))
    return jax.shard_map(
        shards,
        mesh=mesh,
        in_specs=placed,
        out_specs=(P("dp", "mp"), P("dp", None, "mp", None), P("mp", None), P(None, "mp")),
        check_vma=False,
    )
```

```python
import math

import jax
import jax.numpy as jnp
from jax import lax
from jax.experimental import pallas as pl
from jax.experimental.pallas import tpu as pltpu
from jax.sharding import PartitionSpec as P

BF16 = jnp.bfloat16
F32 = jnp.float32
VMEM_LIMIT = 12 * 1024 * 1024

QUAD = 4


def layout_of(dp_count, mp_count):
    depth = dp_count // 2
    pairs = depth // 2

    def member(pair, quad):
        return (quad // 2) * depth + pair * 2 + quad % 2

    window = math.isqrt(pairs)
    quads = [[member(pair, quad) for quad in range(QUAD)] for pair in range(pairs)]
    near = [
        [member(start + index, quad) for index in range(window)]
        for quad in range(QUAD)
        for start in range(0, pairs, window)
    ]
    far = [
        [member(pair, quad) for pair in range(index, pairs, window)]
        for quad in range(QUAD)
        for index in range(window)
    ]
    blocks = [
        [member(pair, quad) * mp_count + index for index in range(mp_count) for quad in range(QUAD)]
        for pair in range(pairs)
    ]
    return quads, near, far, blocks


def call(body, out_shape, *operands, after=()):
    def run(*refs):
        body(*refs[: len(operands)], *refs[len(operands) + len(after) :])

    return pl.pallas_call(
        run,
        out_shape=out_shape,
        in_specs=[
            pl.BlockSpec(memory_space=pltpu.SMEM if operand.ndim == 1 else pltpu.VMEM)
            for operand in operands
        ]
        + [pl.BlockSpec(memory_space=pl.ANY)] * len(after),
        compiler_params=pltpu.CompilerParams(vmem_limit_bytes=VMEM_LIMIT),
    )(*operands, *after)


def contract(left, right, left_dim, right_dim):
    return lax.dot_general(
        left, right, (((left_dim,), (right_dim,)), ((), ())), preferred_element_type=F32
    )


def place_of(quad_ref, step, extent):
    return pl.ds(pl.multiple_of(lax.bitwise_xor(quad_ref[0], step) * extent, extent), extent)


def count_body(ids_ref, counts_ref):
    bag_size, columns = ids_ref.shape
    rows_step, columns_step = 64, 256

    def rows_at(index, carry):
        base = pl.multiple_of(index * rows_step, rows_step)
        rows = lax.broadcasted_iota(jnp.int32, (rows_step, columns_step), 0) + base
        for start in range(0, columns, columns_step):
            span = slice(start, start + columns_step)
            total = jnp.zeros((rows_step, columns_step), F32)
            for slot in range(bag_size):
                total = total + jnp.where(rows == ids_ref[slot : slot + 1, span], 1.0, 0.0)
            counts_ref[pl.ds(base, rows_step), span] = total.astype(BF16)
        return carry

    lax.fori_loop(0, counts_ref.shape[0] // rows_step, rows_at, 0)


def forward_body(
    quad_ref, counts_ref, table_ref, grad0_ref, grad1_ref, grad2_ref, grad3_ref, down_ref, up_ref,
    state_ref, part_ref,
):
    samples = counts_ref.shape[1]
    group = samples // QUAD
    pooled = contract(counts_ref[...], table_ref[...], 0, 0).astype(BF16)
    state_ref[0] = pooled
    for step, one_ref in enumerate((grad0_ref, grad1_ref, grad2_ref, grad3_ref)):
        state_ref[1, step * group : (step + 1) * group, :] = one_ref[...]
    scaled = (state_ref[1].astype(F32) * pooled.astype(F32)).astype(BF16)
    rank_part = contract(pooled, down_ref[...], 1, 0).astype(BF16)
    back_part = contract(scaled, up_ref[...], 1, 1).astype(BF16)
    for step in range(QUAD):
        rows = place_of(quad_ref, step, group)
        part_ref[0, rows, :] = rank_part[step * group : (step + 1) * group]
        part_ref[1, rows, :] = back_part[step * group : (step + 1) * group]


def cross_body(
    quad_ref, ranks_ref, state_ref, down_ref, up_ref,
    parts_ref, back0_ref, back1_ref, back2_ref, back3_ref,
):
    group = state_ref.shape[1] // QUAD

    def in_steps(index):
        return jnp.concatenate(
            [ranks_ref[index, place_of(quad_ref, step, group), :] for step in range(QUAD)], axis=0
        )

    rank_act = in_steps(0)
    rank_grad = in_steps(1)
    pooled = state_ref[0]
    pooled_f = pooled.astype(F32)
    upstream = state_ref[1].astype(F32)
    scaled = (upstream * pooled_f).astype(BF16)
    parts_ref[0] = contract(rank_act, scaled, 0, 0).astype(BF16)
    parts_ref[1] = contract(pooled, rank_grad, 0, 0).astype(BF16)
    scale_map = contract(rank_act, up_ref[...], 1, 0)
    cross = (pooled_f * scale_map + pooled_f).astype(BF16)
    back = contract(rank_grad, down_ref[...], 1, 1)
    pooled_grad = (upstream * scale_map + upstream + back).astype(BF16)
    for step, one_ref in enumerate((back0_ref, back1_ref, back2_ref, back3_ref)):
        one_ref[0] = cross[step * group : (step + 1) * group]
        one_ref[1] = pooled_grad[step * group : (step + 1) * group]


def add_body(slices_ref, copies_ref):
    total = jnp.sum(slices_ref[...].astype(F32), axis=0).astype(BF16)
    for index in range(copies_ref.shape[0]):
        copies_ref[index] = total


def copy_body(value_ref, copies_ref):
    for index in range(copies_ref.shape[0]):
        copies_ref[index] = value_ref[...]


def arrange_body(quad_ref, back0_ref, back1_ref, back2_ref, back3_ref, cross_ref, pooled_grad_ref):
    embed = back0_ref.shape[2]
    for step, one_ref in enumerate((back0_ref, back1_ref, back2_ref, back3_ref)):
        cross_ref[:, place_of(quad_ref, step, embed)] = one_ref[0]
        pooled_grad_ref[lax.bitwise_xor(quad_ref[0], step)] = one_ref[1]


def table_body(order_ref, counts_ref, grads_ref, out_ref):
    count, rows, embed = out_ref.shape
    columns = counts_ref.shape[1]
    group = columns // count
    counts = counts_ref[...].astype(F32)
    tall = jnp.concatenate([counts] * count, axis=0)
    row_of = lax.broadcasted_iota(jnp.int32, tall.shape, 0) // rows
    column_of = lax.broadcasted_iota(jnp.int32, tall.shape, 1) // group
    blocks = jnp.where(row_of == column_of, tall, 0.0).astype(BF16)
    sums = contract(blocks, grads_ref[...].reshape(columns, embed), 1, 0)
    out_ref[...] = sums.astype(BF16).reshape(count, rows, embed)


def sum_tables(order, counts, grads):
    features, group, embed = grads.shape
    rows = counts.shape[0]
    return pl.pallas_call(
        table_body,
        out_shape=shape_of((features, rows, embed)),
        grid_spec=pltpu.PrefetchScalarGridSpec(
            num_scalar_prefetch=1,
            grid=(features // QUAD,),
            in_specs=[
                pl.BlockSpec((rows, QUAD * group), lambda index, order: (0, order[index])),
                pl.BlockSpec((QUAD, group, embed), lambda index, order: (index, 0, 0)),
            ],
            out_specs=pl.BlockSpec((QUAD, rows, embed), lambda index, order: (order[index], 0, 0)),
        ),
        compiler_params=pltpu.CompilerParams(vmem_limit_bytes=VMEM_LIMIT),
    )(order, counts, grads)


def weights_body(sums_ref, down_ref, up_ref):
    width = sums_ref.shape[3]
    for quad in range(QUAD):
        span = slice(quad * width, (quad + 1) * width)
        up_ref[:, span] = sums_ref[quad, 0].astype(F32)
        down_ref[span, :] = sums_ref[quad, 1].astype(F32)


def shape_of(shape, dtype=BF16):
    return jax.ShapeDtypeStruct(shape, dtype)


def shards(bag_ids, tables, down_proj, up_proj, cotangent):
    dp_count, ways = lax.axis_size("dp"), lax.axis_size("mp")
    depth = dp_count // 2
    quads, near, far, blocks = layout_of(dp_count, ways)
    window, windows, members = len(near[0]), len(far[0]), len(blocks[0])
    place = lax.axis_index("dp")
    quad = (place // depth) * 2 + place % 2
    quad_at = quad.reshape(1)
    shard_index = lax.axis_index("mp")
    group, feature_count, bag_size = bag_ids.shape
    _, rows, embed = tables.shape
    rank = down_proj.shape[1]
    samples = QUAD * group

    def exchange(value, axis, groups=None):
        return lax.all_to_all(value, axis, 0, 0, axis_index_groups=groups, tiled=True)

    def swap(values):
        got = [values[0]]
        for step in range(1, QUAD):
            mask = (step // 2) * depth + step % 2
            pairs = [(index, index ^ mask) for index in range(dp_count)]
            got.append(lax.ppermute(values[step], "dp", pairs))
        return got

    def double(value, mask):
        other = lax.ppermute(value, "mp", [(index, index ^ mask) for index in range(ways)])
        return jnp.concatenate([value, other], axis=0)

    with jax.named_scope("inputs"):
        table_parts = lax.dynamic_index_in_dim(
            tables.reshape(ways, QUAD, rows, embed), quad, 1, keepdims=False
        )
        table = exchange(table_parts, "mp").reshape(ways * rows, embed)
        shard_ids = jnp.transpose(
            lax.dynamic_slice_in_dim(bag_ids, shard_index * QUAD, QUAD, 1), (1, 2, 0)
        )
        quad_ids = swap(
            [lax.dynamic_index_in_dim(shard_ids, quad ^ step, 0, keepdims=False) for step in range(QUAD)]
        )
        quad_grads = swap(
            [
                lax.dynamic_slice_in_dim(cotangent, (quad ^ step) * embed, embed, 1)
                for step in range(QUAD)
            ]
        )
        down = lax.dynamic_slice_in_dim(down_proj, quad * embed, embed, 0)
        up = lax.dynamic_slice_in_dim(up_proj, quad * embed, embed, 1)

    with jax.named_scope("counts"):
        quad_counts = call(
            count_body, shape_of((ways * rows, samples)), jnp.concatenate(quad_ids, axis=1)
        )
        row_ids = jnp.transpose(bag_ids, (2, 1, 0)).reshape(bag_size, feature_count * group)
        row_counts = call(
            count_body, shape_of((rows, feature_count * group)), row_ids - shard_index * rows
        )

    with jax.named_scope("forward"):
        state, part = call(
            forward_body, (shape_of((2, samples, embed)), shape_of((2, samples, rank))),
            quad_at, quad_counts, table, *quad_grads, down, up,
        )
    with jax.named_scope("ranks"):
        piece = 2 * samples // members
        pieces = exchange(part.reshape(members, piece, rank), ("dp", "mp"), blocks)
        copies = call(add_body, shape_of((members, piece, rank)), pieces, after=(row_counts,))
        ranks = exchange(copies, ("dp", "mp"), blocks).reshape(2, samples, rank)

    with jax.named_scope("cross"):
        parts, *backs = call(
            cross_body, (shape_of((2, embed, rank)),) + (shape_of((2, group, embed)),) * QUAD,
            quad_at, ranks, state, down, up,
        )

    slab = (2 * embed // window, rank)
    with jax.named_scope("near_sums"):
        near_parts = exchange(parts.reshape((window,) + slab), "dp", near)
        cross_out, grads = call(
            arrange_body, (shape_of((group, QUAD * embed)), shape_of((QUAD, group, embed))),
            quad_at, *swap(backs),
        )
        near_copies = call(add_body, shape_of((windows,) + slab), near_parts, after=(grads,))
    with jax.named_scope("far_sums"):
        far_parts = exchange(near_copies, "dp", far)
        steps = [ways >> (index + 1) for index in range(ways.bit_length() - 1)]
        for mask in steps[:-2]:
            grads = double(grads, mask)
        far_copies = call(add_body, shape_of((window,) + slab), far_parts, after=(grads,))
    with jax.named_scope("near_gather"):
        sums = exchange(far_copies, "dp", near)
        grads = double(grads, steps[-2])
        quad_copies = call(
            copy_body, shape_of((QUAD, window) + slab), sums, after=(grads,)
        )
    with jax.named_scope("quad_gather"):
        every = exchange(quad_copies, "dp", quads).reshape(QUAD, 2, embed, rank)
        grads = double(grads, steps[-1])
        order = [shard_index]
        for mask in steps:
            order = order + [index ^ mask for index in order]
        table_grads = sum_tables(jnp.stack(order), row_counts, grads)[None]
        down_grad, up_grad = call(
            weights_body, (shape_of(down_proj.shape, F32), shape_of(up_proj.shape, F32)), every
        )
    return (cross_out, table_grads, down_grad, up_grad)


def solution(mesh):
    placed = (P("dp", None, None), P(None, "mp", None), P("mp", None), P(None, "mp"), P("dp", "mp"))
    return jax.shard_map(
        shards,
        mesh=mesh,
        in_specs=placed,
        out_specs=(P("dp", "mp"), P("dp", None, "mp", None), P("mp", None), P(None, "mp")),
        check_vma=False,
    )
```

```python
import math

import jax
import jax.numpy as jnp
from jax import lax
from jax.experimental import pallas as pl
from jax.experimental.pallas import tpu as pltpu
from jax.sharding import PartitionSpec as P

BF16 = jnp.bfloat16
F32 = jnp.float32
VMEM_LIMIT = 12 * 1024 * 1024

QUAD = 4
ID_BITS = 5


def layout_of(dp_count, mp_count):
    depth = dp_count // 2
    pairs = depth // 2

    def member(pair, quad):
        return (quad // 2) * depth + pair * 2 + quad % 2

    window = math.isqrt(pairs)
    quads = [[member(pair, quad) for quad in range(QUAD)] for pair in range(pairs)]
    near = [
        [member(start + index, quad) for index in range(window)]
        for quad in range(QUAD)
        for start in range(0, pairs, window)
    ]
    far = [
        [member(pair, quad) for pair in range(index, pairs, window)]
        for quad in range(QUAD)
        for index in range(window)
    ]
    blocks = [
        [member(pair, quad) * mp_count + index for index in range(mp_count) for quad in range(QUAD)]
        for pair in range(pairs)
    ]
    return quads, near, far, blocks


def call(body, out_shape, *operands, after=()):
    def run(*refs):
        body(*refs[: len(operands)], *refs[len(operands) + len(after) :])

    return pl.pallas_call(
        run,
        out_shape=out_shape,
        in_specs=[
            pl.BlockSpec(memory_space=pltpu.SMEM if operand.ndim == 1 else pltpu.VMEM)
            for operand in operands
        ]
        + [pl.BlockSpec(memory_space=pl.ANY)] * len(after),
        compiler_params=pltpu.CompilerParams(vmem_limit_bytes=VMEM_LIMIT),
    )(*operands, *after)


def contract(left, right, left_dim, right_dim):
    return lax.dot_general(
        left, right, (((left_dim,), (right_dim,)), ((), ())), preferred_element_type=F32
    )


def place_of(quad_ref, step, extent):
    return pl.ds(pl.multiple_of(lax.bitwise_xor(quad_ref[0], step) * extent, extent), extent)


def count_of(ids, base, rows):
    slots = lax.broadcasted_iota(jnp.int32, (rows, ids.shape[1]), 0) + base
    total = jnp.zeros(slots.shape, F32)
    for slot in range(ids.shape[0]):
        total = total + jnp.where(slots == ids[slot : slot + 1, :], 1.0, 0.0)
    return total


def pack_body(quad_ref, shard_ref, ids_ref, grad_ref, *packed_refs):
    group, width = grad_ref.shape
    bag_size = ids_ref.shape[0]
    embed = width // QUAD
    span = QUAD * group
    own = ids_ref[:, pl.ds(pl.multiple_of(shard_ref[0] * span, span), span)]
    high = lax.shift_right_logical(own, ID_BITS).astype(F32).astype(BF16)
    low = lax.bitwise_and(own, (1 << ID_BITS) - 1).astype(F32).astype(BF16)
    for step, packed_ref in enumerate(packed_refs):
        packed_ref[:group, :] = grad_ref[:, place_of(quad_ref, step, embed)]
        packed_ref[group : group + bag_size, :] = high
        packed_ref[group + bag_size :, :] = low


def count_body(quad_ref, *refs):
    packed_refs, counts_ref, grad_ref = refs[:-2], refs[-2], refs[-1]
    columns = counts_ref.shape[1]
    group = columns // QUAD
    bag_size = (packed_refs[0].shape[0] - group) // 2
    lanes = lax.broadcasted_iota(jnp.int32, (bag_size, columns), 1)
    ids = jnp.zeros((bag_size, columns), jnp.int32)
    for step, packed_ref in enumerate(packed_refs):
        grad_ref[step * group : (step + 1) * group, :] = packed_ref[:group, :]
        high = packed_ref[group : group + bag_size, :].astype(F32)
        low = packed_ref[group + bag_size :, :].astype(F32)
        every = (high * (1 << ID_BITS) + low).astype(jnp.int32)
        turn = lax.bitwise_and(step - quad_ref[0], QUAD - 1) * group
        here = (lanes >= step * group) & (lanes < (step + 1) * group)
        ids = jnp.where(here, pltpu.roll(every, turn, 1), ids)
    rows = 64

    def rows_at(index, carry):
        base = pl.multiple_of(index * rows, rows)
        counts_ref[pl.ds(base, rows), :] = count_of(ids, base, rows).astype(BF16)
        return carry

    lax.fori_loop(0, counts_ref.shape[0] // rows, rows_at, 0)


def block_body(order_ref, ids_ref, blocks_ref, done_ref):
    shards_of, width, _ = blocks_ref.shape
    rows = width // QUAD
    row_of = lax.broadcasted_iota(jnp.int32, (width, width), 0) // rows
    column_of = lax.broadcasted_iota(jnp.int32, (width, width), 1) // rows

    def shard_at(index, carry):
        start = pl.multiple_of(order_ref[index] * width, width)
        counts = count_of(ids_ref[:, pl.ds(start, width)], order_ref[0] * rows, rows)
        tall = jnp.concatenate([counts] * QUAD, axis=0)
        blocks_ref[index] = jnp.where(row_of == column_of, tall, 0.0).astype(BF16)
        return carry

    lax.fori_loop(0, shards_of, shard_at, 0)
    done_ref[...] = jnp.zeros(done_ref.shape, done_ref.dtype)


def forward_body(
    quad_ref, counts_ref, grad_ref, table_ref, down_ref, up_ref, state_ref, part_ref,
):
    samples = counts_ref.shape[1]
    group = samples // QUAD
    pooled = contract(counts_ref[...], table_ref[...], 0, 0).astype(BF16)
    state_ref[0] = pooled
    state_ref[1] = grad_ref[...]
    scaled = (grad_ref[...].astype(F32) * pooled.astype(F32)).astype(BF16)
    rank_part = contract(pooled, down_ref[...], 1, 0).astype(BF16)
    back_part = contract(scaled, up_ref[...], 1, 1).astype(BF16)
    for step in range(QUAD):
        rows = place_of(quad_ref, step, group)
        part_ref[0, rows, :] = rank_part[step * group : (step + 1) * group]
        part_ref[1, rows, :] = back_part[step * group : (step + 1) * group]


def cross_body(
    quad_ref, ranks_ref, state_ref, down_ref, up_ref,
    parts_ref, back0_ref, back1_ref, back2_ref, back3_ref,
):
    group = state_ref.shape[1] // QUAD

    def in_steps(index):
        return jnp.concatenate(
            [ranks_ref[index, place_of(quad_ref, step, group), :] for step in range(QUAD)], axis=0
        )

    rank_act = in_steps(0)
    rank_grad = in_steps(1)
    pooled = state_ref[0]
    pooled_f = pooled.astype(F32)
    upstream = state_ref[1].astype(F32)
    scaled = (upstream * pooled_f).astype(BF16)
    parts_ref[0] = contract(rank_act, scaled, 0, 0).astype(BF16)
    parts_ref[1] = contract(pooled, rank_grad, 0, 0).astype(BF16)
    scale_map = contract(rank_act, up_ref[...], 1, 0)
    cross = (pooled_f * scale_map + pooled_f).astype(BF16)
    back = contract(rank_grad, down_ref[...], 1, 1)
    pooled_grad = (upstream * scale_map + upstream + back).astype(BF16)
    for step, one_ref in enumerate((back0_ref, back1_ref, back2_ref, back3_ref)):
        one_ref[0] = cross[step * group : (step + 1) * group]
        one_ref[1] = pooled_grad[step * group : (step + 1) * group]


def add_body(slices_ref, copies_ref):
    total = jnp.sum(slices_ref[...].astype(F32), axis=0).astype(BF16)
    for index in range(copies_ref.shape[0]):
        copies_ref[index] = total


def copy_body(value_ref, copies_ref):
    for index in range(copies_ref.shape[0]):
        copies_ref[index] = value_ref[...]


def arrange_body(quad_ref, back0_ref, back1_ref, back2_ref, back3_ref, cross_ref, pooled_grad_ref):
    embed = back0_ref.shape[2]
    for step, one_ref in enumerate((back0_ref, back1_ref, back2_ref, back3_ref)):
        cross_ref[:, place_of(quad_ref, step, embed)] = one_ref[0]
        pooled_grad_ref[lax.bitwise_xor(quad_ref[0], step)] = one_ref[1]


def table_body(order_ref, blocks_ref, grads_ref, out_ref):
    count, width, _ = blocks_ref.shape
    _, rows, embed = out_ref.shape
    first = pl.program_id(0) * count
    for index in range(count):
        grads = grads_ref[index * QUAD : (index + 1) * QUAD].reshape(width, embed)
        sums = contract(blocks_ref[index], grads, 1, 0).astype(BF16)
        start = order_ref[first + index] * QUAD
        for feature in range(QUAD):
            out_ref[start + feature] = sums[feature * rows : (feature + 1) * rows]


def sum_tables(order, blocks, grads):
    features, group, embed = grads.shape
    shards_of, width, _ = blocks.shape
    count = shards_of // 4
    out = (features, width // QUAD, embed)
    return pl.pallas_call(
        table_body,
        out_shape=shape_of(out),
        grid_spec=pltpu.PrefetchScalarGridSpec(
            num_scalar_prefetch=1,
            grid=(4,),
            in_specs=[
                pl.BlockSpec((count, width, width), lambda index, order: (index, 0, 0)),
                pl.BlockSpec((count * QUAD, group, embed), lambda index, order: (index, 0, 0)),
            ],
            out_specs=pl.BlockSpec(out, lambda index, order: (0, 0, 0)),
        ),
        compiler_params=pltpu.CompilerParams(vmem_limit_bytes=VMEM_LIMIT),
    )(order, blocks, grads)


def weights_body(sums_ref, down_ref, up_ref):
    width = sums_ref.shape[3]
    for quad in range(QUAD):
        span = slice(quad * width, (quad + 1) * width)
        up_ref[:, span] = sums_ref[quad, 0].astype(F32)
        down_ref[span, :] = sums_ref[quad, 1].astype(F32)


def shape_of(shape, dtype=BF16):
    return jax.ShapeDtypeStruct(shape, dtype)


def shards(bag_ids, tables, down_proj, up_proj, cotangent):
    dp_count, ways = lax.axis_size("dp"), lax.axis_size("mp")
    depth = dp_count // 2
    quads, near, far, blocks = layout_of(dp_count, ways)
    window, windows, members = len(near[0]), len(far[0]), len(blocks[0])
    place = lax.axis_index("dp")
    quad = (place // depth) * 2 + place % 2
    quad_at = quad.reshape(1)
    shard_index = lax.axis_index("mp")
    group, feature_count, bag_size = bag_ids.shape
    _, rows, embed = tables.shape
    rank = down_proj.shape[1]
    samples = QUAD * group

    def exchange(value, axis, groups=None):
        return lax.all_to_all(value, axis, 0, 0, axis_index_groups=groups, tiled=True)

    def swap(values):
        got = [values[0]]
        for step in range(1, QUAD):
            mask = (step // 2) * depth + step % 2
            pairs = [(index, index ^ mask) for index in range(dp_count)]
            got.append(lax.ppermute(values[step], "dp", pairs))
        return got

    def double(value, mask):
        other = lax.ppermute(value, "mp", [(index, index ^ mask) for index in range(ways)])
        return jnp.concatenate([value, other], axis=0)

    with jax.named_scope("inputs"):
        table_parts = lax.dynamic_index_in_dim(
            tables.reshape(ways, QUAD, rows, embed), quad, 1, keepdims=False
        )
        table = exchange(table_parts, "mp").reshape(ways * rows, embed)
        ids = jnp.transpose(bag_ids, (2, 1, 0)).reshape(bag_size, feature_count * group)
        packed_shape = shape_of((group + 2 * bag_size, embed))
        packed = swap(
            call(pack_body, (packed_shape,) * QUAD, quad_at, shard_index.reshape(1), ids, cotangent)
        )
        down = lax.dynamic_slice_in_dim(down_proj, quad * embed, embed, 0)
        up = lax.dynamic_slice_in_dim(up_proj, quad * embed, embed, 1)

    with jax.named_scope("counts"):
        quad_counts, grad = call(
            count_body, (shape_of((ways * rows, samples)), shape_of((samples, embed))), quad_at, *packed
        )
        steps = [ways >> (index + 1) for index in range(ways.bit_length() - 1)]
        order = [shard_index]
        for mask in steps:
            order = order + [index ^ mask for index in order]
        order = jnp.stack(order)
        row_blocks, done = call(
            block_body, (shape_of((ways, QUAD * rows, QUAD * group)), shape_of((8, 128), F32)), order, ids
        )

    with jax.named_scope("forward"):
        state, part = call(
            forward_body, (shape_of((2, samples, embed)), shape_of((2, samples, rank))),
            quad_at, quad_counts, grad, table, down, up,
        )
    with jax.named_scope("ranks"):
        piece = 2 * samples // members
        pieces = exchange(part.reshape(members, piece, rank), ("dp", "mp"), blocks)
        copies = call(add_body, shape_of((members, piece, rank)), pieces, after=(done,))
        ranks = exchange(copies, ("dp", "mp"), blocks).reshape(2, samples, rank)

    with jax.named_scope("cross"):
        parts, *backs = call(
            cross_body, (shape_of((2, embed, rank)),) + (shape_of((2, group, embed)),) * QUAD,
            quad_at, ranks, state, down, up,
        )

    slab = (2 * embed // window, rank)
    with jax.named_scope("near_sums"):
        near_parts = exchange(parts.reshape((window,) + slab), "dp", near)
        cross_out, grads = call(
            arrange_body, (shape_of((group, QUAD * embed)), shape_of((QUAD, group, embed))),
            quad_at, *swap(backs),
        )
        near_copies = call(add_body, shape_of((windows,) + slab), near_parts, after=(grads,))
    with jax.named_scope("far_sums"):
        far_parts = exchange(near_copies, "dp", far)
        for mask in steps[:-1]:
            grads = double(grads, mask)
        far_copies = call(add_body, shape_of((window,) + slab), far_parts, after=(grads,))
    with jax.named_scope("near_gather"):
        sums = exchange(far_copies, "dp", near)
        grads = double(grads, steps[-1])
        quad_copies = call(
            copy_body, shape_of((QUAD, window) + slab), sums, after=(grads,)
        )
    with jax.named_scope("quad_gather"):
        every = exchange(quad_copies, "dp", quads).reshape(QUAD, 2, embed, rank)
        table_grads = sum_tables(order, row_blocks, grads)[None]
        down_grad, up_grad = call(
            weights_body, (shape_of(down_proj.shape, F32), shape_of(up_proj.shape, F32)), every
        )
    return (cross_out, table_grads, down_grad, up_grad)


def solution(mesh):
    placed = (P("dp", None, None), P(None, "mp", None), P("mp", None), P(None, "mp"), P("dp", "mp"))
    return jax.shard_map(
        shards,
        mesh=mesh,
        in_specs=placed,
        out_specs=(P("dp", "mp"), P("dp", None, "mp", None), P("mp", None), P(None, "mp")),
        check_vma=False,
    )
```

```python
import math

import jax
import jax.numpy as jnp
from jax import lax
from jax.experimental import pallas as pl
from jax.experimental.pallas import tpu as pltpu
from jax.sharding import PartitionSpec as P

BF16 = jnp.bfloat16
F32 = jnp.float32
VMEM_LIMIT = 12 * 1024 * 1024

QUAD = 4
ID_BITS = 5


def layout_of(dp_count, mp_count):
    depth = dp_count // 2
    pairs = depth // 2

    def member(pair, quad):
        return (quad // 2) * depth + pair * 2 + quad % 2

    window = math.isqrt(pairs)
    quads = [[member(pair, quad) for quad in range(QUAD)] for pair in range(pairs)]
    near = [
        [member(start + index, quad) for index in range(window)]
        for quad in range(QUAD)
        for start in range(0, pairs, window)
    ]
    far = [
        [member(pair, quad) for pair in range(index, pairs, window)]
        for quad in range(QUAD)
        for index in range(window)
    ]
    blocks = [
        [member(pair, quad) * mp_count + index for index in range(mp_count) for quad in range(QUAD)]
        for pair in range(pairs)
    ]
    return quads, near, far, blocks


def call(body, out_shape, *operands, after=()):
    def run(*refs):
        body(*refs[: len(operands)], *refs[len(operands) + len(after) :])

    return pl.pallas_call(
        run,
        out_shape=out_shape,
        in_specs=[
            pl.BlockSpec(memory_space=pltpu.SMEM if operand.ndim == 1 else pltpu.VMEM)
            for operand in operands
        ]
        + [pl.BlockSpec(memory_space=pl.ANY)] * len(after),
        compiler_params=pltpu.CompilerParams(vmem_limit_bytes=VMEM_LIMIT),
    )(*operands, *after)


def call_sliced(body, out_shape, quad_at, operands, sliced, scratch=(), limit=VMEM_LIMIT):
    def whole(array):
        return pl.BlockSpec(array.shape, lambda index, quad: (0,) * len(array.shape))

    def part(array, dim):
        shape = list(array.shape)
        shape[dim] //= QUAD
        return pl.BlockSpec(
            tuple(shape),
            lambda index, quad: tuple(quad[0] if axis == dim else 0 for axis in range(len(shape))),
        )

    return pl.pallas_call(
        body,
        out_shape=out_shape,
        grid_spec=pltpu.PrefetchScalarGridSpec(
            num_scalar_prefetch=1,
            grid=(1,),
            in_specs=[whole(operand) for operand in operands] + [part(*pair) for pair in sliced],
            out_specs=jax.tree.map(whole, out_shape),
            scratch_shapes=scratch,
        ),
        compiler_params=pltpu.CompilerParams(vmem_limit_bytes=limit),
    )(quad_at, *operands, *(array for array, _ in sliced))


def contract(left, right, left_dim, right_dim):
    return lax.dot_general(
        left, right, (((left_dim,), (right_dim,)), ((), ())), preferred_element_type=F32
    )


def place_of(quad_ref, step, extent):
    return pl.ds(pl.multiple_of(lax.bitwise_xor(quad_ref[0], step) * extent, extent), extent)


def count_of(ids, base, rows):
    slots = lax.broadcasted_iota(jnp.int32, (rows, ids.shape[1]), 0) + base
    total = jnp.zeros(slots.shape, F32)
    for slot in range(ids.shape[0]):
        total = total + jnp.where(slots == ids[slot : slot + 1, :], 1.0, 0.0)
    return total


def slice_body(quad_ref, source_ref, slice_ref):
    slice_ref[...] = source_ref[:, 0]


def pack_body(quad_ref, shard_ref, ids_ref, grad_ref, *packed_refs):
    group, width = grad_ref.shape
    bag_size = ids_ref.shape[0]
    embed = width // QUAD
    span = QUAD * group
    own = ids_ref[:, pl.ds(pl.multiple_of(shard_ref[0] * span, span), span)]
    high = lax.shift_right_logical(own, ID_BITS).astype(F32).astype(BF16)
    low = lax.bitwise_and(own, (1 << ID_BITS) - 1).astype(F32).astype(BF16)
    for step, packed_ref in enumerate(packed_refs):
        packed_ref[:group, :] = grad_ref[:, place_of(quad_ref, step, embed)]
        packed_ref[group : group + bag_size, :] = high
        packed_ref[group + bag_size :, :] = low


def ids_of(quad_ref, packed_refs, columns):
    group = columns // QUAD
    bag_size = (packed_refs[0].shape[0] - group) // 2
    lanes = lax.broadcasted_iota(jnp.int32, (bag_size, columns), 1)
    ids = jnp.zeros((bag_size, columns), jnp.int32)
    for step, packed_ref in enumerate(packed_refs):
        high = packed_ref[group : group + bag_size, :].astype(F32)
        low = packed_ref[group + bag_size :, :].astype(F32)
        every = (high * (1 << ID_BITS) + low).astype(jnp.int32)
        turn = lax.bitwise_and(step - quad_ref[0], QUAD - 1) * group
        here = (lanes >= step * group) & (lanes < (step + 1) * group)
        ids = jnp.where(here, pltpu.roll(every, turn, 1), ids)
    return ids


def block_body(shard_ref, ids_ref, blocks_ref, done_ref):
    shards_of, width, _ = blocks_ref.shape
    rows = width // QUAD
    row_of = lax.broadcasted_iota(jnp.int32, (width, width), 0) // rows
    column_of = lax.broadcasted_iota(jnp.int32, (width, width), 1) // rows

    def shard_at(index, carry):
        start = pl.multiple_of(index * width, width)
        counts = count_of(ids_ref[:, pl.ds(start, width)], shard_ref[0] * rows, rows)
        tall = jnp.concatenate([counts] * QUAD, axis=0)
        blocks_ref[index] = jnp.where(row_of == column_of, tall, 0.0).astype(BF16)
        return carry

    lax.fori_loop(0, shards_of, shard_at, 0)
    done_ref[...] = jnp.zeros(done_ref.shape, done_ref.dtype)


def forward_body(
    quad_ref, table_ref, packed0_ref, packed1_ref, packed2_ref, packed3_ref, down_ref, up_ref,
    state_ref, part_ref, ids_ref, counts_ref,
):
    packed_refs = (packed0_ref, packed1_ref, packed2_ref, packed3_ref)
    samples = state_ref.shape[1]
    group = samples // QUAD
    rows = 64
    ids_ref[...] = ids_of(quad_ref, packed_refs, samples)

    def rows_at(index, carry):
        base = pl.multiple_of(index * rows, rows)
        counts_ref[pl.ds(base, rows), :] = count_of(ids_ref[...], base, rows).astype(BF16)
        return carry

    lax.fori_loop(0, counts_ref.shape[0] // rows, rows_at, 0)
    pooled = contract(counts_ref[...], table_ref[...], 0, 0).astype(BF16)
    state_ref[0] = pooled
    for step, packed_ref in enumerate(packed_refs):
        state_ref[1, step * group : (step + 1) * group, :] = packed_ref[:group, :]
    scaled = (state_ref[1].astype(F32) * pooled.astype(F32)).astype(BF16)
    rank_part = contract(pooled, down_ref[...], 1, 0).astype(BF16)
    back_part = contract(scaled, up_ref[...], 1, 1).astype(BF16)
    for step in range(QUAD):
        rows_of = place_of(quad_ref, step, group)
        part_ref[0, rows_of, :] = rank_part[step * group : (step + 1) * group]
        part_ref[1, rows_of, :] = back_part[step * group : (step + 1) * group]


def cross_body(
    quad_ref, ranks_ref, state_ref, down_ref, up_ref,
    parts_ref, back0_ref, back1_ref, back2_ref, back3_ref,
):
    group = state_ref.shape[1] // QUAD

    def in_steps(index):
        return jnp.concatenate(
            [ranks_ref[index, place_of(quad_ref, step, group), :] for step in range(QUAD)], axis=0
        )

    rank_act = in_steps(0)
    rank_grad = in_steps(1)
    pooled = state_ref[0]
    pooled_f = pooled.astype(F32)
    upstream = state_ref[1].astype(F32)
    scaled = (upstream * pooled_f).astype(BF16)
    parts_ref[0] = contract(rank_act, scaled, 0, 0).astype(BF16)
    parts_ref[1] = contract(pooled, rank_grad, 0, 0).astype(BF16)
    scale_map = contract(rank_act, up_ref[...], 1, 0)
    cross = (pooled_f * scale_map + pooled_f).astype(BF16)
    back = contract(rank_grad, down_ref[...], 1, 1)
    pooled_grad = (upstream * scale_map + upstream + back).astype(BF16)
    for step, one_ref in enumerate((back0_ref, back1_ref, back2_ref, back3_ref)):
        one_ref[0] = cross[step * group : (step + 1) * group]
        one_ref[1] = pooled_grad[step * group : (step + 1) * group]


def add_body(slices_ref, copies_ref):
    total = jnp.sum(slices_ref[...].astype(F32), axis=0).astype(BF16)
    for index in range(copies_ref.shape[0]):
        copies_ref[index] = total


def copy_body(value_ref, copies_ref):
    for index in range(copies_ref.shape[0]):
        copies_ref[index] = value_ref[...]


def arrange_body(quad_ref, back0_ref, back1_ref, back2_ref, back3_ref, cross_ref, pooled_grad_ref):
    embed = back0_ref.shape[2]
    for step, one_ref in enumerate((back0_ref, back1_ref, back2_ref, back3_ref)):
        cross_ref[:, place_of(quad_ref, step, embed)] = one_ref[0]
        pooled_grad_ref[lax.bitwise_xor(quad_ref[0], step)] = one_ref[1]


def table_body(blocks_ref, grads_ref, out_ref):
    count, width, _ = blocks_ref.shape
    _, rows, embed = out_ref.shape
    for index in range(count):
        features = slice(index * QUAD, (index + 1) * QUAD)
        grads = grads_ref[features].reshape(width, embed)
        sums = contract(blocks_ref[index], grads, 1, 0).astype(BF16)
        out_ref[features] = sums.reshape(QUAD, rows, embed)


def sum_tables(blocks, grads):
    features, group, embed = grads.shape
    shards_of, width, _ = blocks.shape
    rows = width // QUAD
    count = shards_of // 4

    def block(*shape):
        return pl.BlockSpec(shape, lambda index: (index, 0, 0))

    return pl.pallas_call(
        table_body,
        out_shape=shape_of((features, rows, embed)),
        grid=(4,),
        in_specs=[block(count, width, width), block(count * QUAD, group, embed)],
        out_specs=block(count * QUAD, rows, embed),
        compiler_params=pltpu.CompilerParams(vmem_limit_bytes=VMEM_LIMIT),
    )(blocks, grads)


def weights_body(sums_ref, down_ref, up_ref):
    width = sums_ref.shape[3]
    for quad in range(QUAD):
        span = slice(quad * width, (quad + 1) * width)
        up_ref[:, span] = sums_ref[quad, 0].astype(F32)
        down_ref[span, :] = sums_ref[quad, 1].astype(F32)


def shape_of(shape, dtype=BF16):
    return jax.ShapeDtypeStruct(shape, dtype)


def shards(bag_ids, tables, down_proj, up_proj, cotangent):
    dp_count, ways = lax.axis_size("dp"), lax.axis_size("mp")
    depth = dp_count // 2
    quads, near, far, blocks = layout_of(dp_count, ways)
    window, windows, members = len(near[0]), len(far[0]), len(blocks[0])
    place = lax.axis_index("dp")
    quad = (place // depth) * 2 + place % 2
    quad_at = quad.reshape(1)
    shard_index = lax.axis_index("mp")
    group, feature_count, bag_size = bag_ids.shape
    _, rows, embed = tables.shape
    rank = down_proj.shape[1]
    samples = QUAD * group

    def exchange(value, axis, groups=None):
        return lax.all_to_all(value, axis, 0, 0, axis_index_groups=groups, tiled=True)

    def swap(values):
        got = [values[0]]
        for step in range(1, QUAD):
            mask = (step // 2) * depth + step % 2
            pairs = [(index, index ^ mask) for index in range(dp_count)]
            got.append(lax.ppermute(values[step], "dp", pairs))
        return got

    with jax.named_scope("inputs"):
        table_parts = call_sliced(
            slice_body, shape_of((ways, rows, embed)), quad_at, (),
            ((tables.reshape(ways, QUAD, rows, embed), 1),), limit=5 * VMEM_LIMIT,
        )
        table = exchange(table_parts, "mp").reshape(ways * rows, embed)
        ids = jnp.transpose(bag_ids, (2, 1, 0)).reshape(bag_size, feature_count * group)
        packed_shape = shape_of((group + 2 * bag_size, embed))
        packed = swap(
            call(pack_body, (packed_shape,) * QUAD, quad_at, shard_index.reshape(1), ids, cotangent)
        )
        weights = ((down_proj, 0), (up_proj, 1))

    with jax.named_scope("counts"):
        row_blocks, done = call(
            block_body, (shape_of((ways, QUAD * rows, QUAD * group)), shape_of((8, 128), F32)), shard_index.reshape(1), ids
        )

    with jax.named_scope("forward"):
        state, part = call_sliced(
            forward_body, (shape_of((2, samples, embed)), shape_of((2, samples, rank))),
            quad_at, (table, *packed), weights,
            (pltpu.VMEM((bag_size, samples), jnp.int32), pltpu.VMEM((ways * rows, samples), BF16)),
        )
    with jax.named_scope("ranks"):
        piece = 2 * samples // members
        pieces = exchange(part.reshape(members, piece, rank), ("dp", "mp"), blocks)
        copies = call(add_body, shape_of((members, piece, rank)), pieces, after=(done,))
        ranks = exchange(copies, ("dp", "mp"), blocks).reshape(2, samples, rank)

    with jax.named_scope("cross"):
        parts, *backs = call_sliced(
            cross_body, (shape_of((2, embed, rank)),) + (shape_of((2, group, embed)),) * QUAD,
            quad_at, (ranks, state), weights,
        )

    slab = (2 * embed // window, rank)
    with jax.named_scope("near_sums"):
        near_parts = exchange(parts.reshape((window,) + slab), "dp", near)
        cross_out, grads = call(
            arrange_body, (shape_of((group, QUAD * embed)), shape_of((QUAD, group, embed))),
            quad_at, *swap(backs),
        )
        near_copies = call(add_body, shape_of((windows,) + slab), near_parts, after=(grads,))
        every_grad = lax.all_gather(grads, "mp", axis=0, tiled=True)
    with jax.named_scope("far_sums"):
        far_parts = exchange(near_copies, "dp", far)
        far_copies = call(add_body, shape_of((window,) + slab), far_parts)
    with jax.named_scope("near_gather"):
        sums = exchange(far_copies, "dp", near)
        quad_copies = call(
            copy_body, shape_of((QUAD, window) + slab), sums, after=(every_grad,)
        )
    with jax.named_scope("quad_gather"):
        every = exchange(quad_copies, "dp", quads).reshape(QUAD, 2, embed, rank)
        table_grads = sum_tables(row_blocks, every_grad)[None]
        down_grad, up_grad = call(
            weights_body, (shape_of(down_proj.shape, F32), shape_of(up_proj.shape, F32)), every
        )
    return (cross_out, table_grads, down_grad, up_grad)


def solution(mesh):
    placed = (P("dp", None, None), P(None, "mp", None), P("mp", None), P(None, "mp"), P("dp", "mp"))
    return jax.shard_map(
        shards,
        mesh=mesh,
        in_specs=placed,
        out_specs=(P("dp", "mp"), P("dp", None, "mp", None), P("mp", None), P(None, "mp")),
        check_vma=False,
    )
```

```python
import jax
import jax.numpy as jnp
from jax import lax
from jax.experimental import pallas as pl
from jax.experimental.pallas import tpu as pltpu
from jax.sharding import PartitionSpec as P

BF16 = jnp.bfloat16
F32 = jnp.float32
VMEM_LIMIT = 12 * 1024 * 1024

QUAD = 4
ID_BITS = 5


def layout_of(dp_count, mp_count):
    depth = dp_count // 2
    pairs = depth // 2

    def member(pair, quad):
        return (quad // 2) * depth + pair * 2 + quad % 2

    quads = [[member(pair, quad) for quad in range(QUAD)] for pair in range(pairs)]
    lines = [[member(pair, quad) for pair in range(pairs)] for quad in range(QUAD)]
    blocks = [
        [member(pair, quad) * mp_count + index for index in range(mp_count) for quad in range(QUAD)]
        for pair in range(pairs)
    ]
    return quads, lines, blocks


def call(body, out_shape, *operands, after=()):
    def run(*refs):
        body(*refs[: len(operands)], *refs[len(operands) + len(after) :])

    return pl.pallas_call(
        run,
        out_shape=out_shape,
        in_specs=[
            pl.BlockSpec(memory_space=pltpu.SMEM if operand.ndim == 1 else pltpu.VMEM)
            for operand in operands
        ]
        + [pl.BlockSpec(memory_space=pl.ANY)] * len(after),
        compiler_params=pltpu.CompilerParams(vmem_limit_bytes=VMEM_LIMIT),
    )(*operands, *after)


def call_sliced(body, out_shape, quad_at, operands, sliced, scratch=(), limit=VMEM_LIMIT):
    def whole(array):
        return pl.BlockSpec(array.shape, lambda index, quad: (0,) * len(array.shape))

    def part(array, dim):
        shape = list(array.shape)
        shape[dim] //= QUAD
        return pl.BlockSpec(
            tuple(shape),
            lambda index, quad: tuple(quad[0] if axis == dim else 0 for axis in range(len(shape))),
        )

    return pl.pallas_call(
        body,
        out_shape=out_shape,
        grid_spec=pltpu.PrefetchScalarGridSpec(
            num_scalar_prefetch=1,
            grid=(1,),
            in_specs=[whole(operand) for operand in operands] + [part(*pair) for pair in sliced],
            out_specs=jax.tree.map(whole, out_shape),
            scratch_shapes=scratch,
        ),
        compiler_params=pltpu.CompilerParams(vmem_limit_bytes=limit),
    )(quad_at, *operands, *(array for array, _ in sliced))


def contract(left, right, left_dim, right_dim):
    return lax.dot_general(
        left, right, (((left_dim,), (right_dim,)), ((), ())), preferred_element_type=F32
    )


def place_of(quad_ref, step, extent):
    return pl.ds(pl.multiple_of(lax.bitwise_xor(quad_ref[0], step) * extent, extent), extent)


def count_of(ids, base, rows):
    slots = lax.broadcasted_iota(jnp.int32, (rows, ids.shape[1]), 0) + base
    total = jnp.zeros(slots.shape, F32)
    for slot in range(ids.shape[0]):
        total = total + jnp.where(slots == ids[slot : slot + 1, :], 1.0, 0.0)
    return total


def slice_body(quad_ref, source_ref, slice_ref):
    slice_ref[...] = source_ref[:, 0]


def pack_body(quad_ref, shard_ref, ids_ref, grad_ref, *packed_refs):
    group, width = grad_ref.shape
    bag_size = ids_ref.shape[0]
    embed = width // QUAD
    span = QUAD * group
    own = ids_ref[:, pl.ds(pl.multiple_of(shard_ref[0] * span, span), span)]
    high = lax.shift_right_logical(own, ID_BITS).astype(F32).astype(BF16)
    low = lax.bitwise_and(own, (1 << ID_BITS) - 1).astype(F32).astype(BF16)
    for step, packed_ref in enumerate(packed_refs):
        packed_ref[:group, :] = grad_ref[:, place_of(quad_ref, step, embed)]
        packed_ref[group : group + bag_size, :] = high
        packed_ref[group + bag_size :, :] = low


def ids_of(quad_ref, packed_refs, columns):
    group = columns // QUAD
    bag_size = (packed_refs[0].shape[0] - group) // 2
    lanes = lax.broadcasted_iota(jnp.int32, (bag_size, columns), 1)
    ids = jnp.zeros((bag_size, columns), jnp.int32)
    for step, packed_ref in enumerate(packed_refs):
        high = packed_ref[group : group + bag_size, :].astype(F32)
        low = packed_ref[group + bag_size :, :].astype(F32)
        every = (high * (1 << ID_BITS) + low).astype(jnp.int32)
        turn = lax.bitwise_and(step - quad_ref[0], QUAD - 1) * group
        here = (lanes >= step * group) & (lanes < (step + 1) * group)
        ids = jnp.where(here, pltpu.roll(every, turn, 1), ids)
    return ids


def block_body(order_ref, ids_ref, blocks_ref, done_ref):
    shards_of, width, _ = blocks_ref.shape
    rows = width // QUAD
    row_of = lax.broadcasted_iota(jnp.int32, (width, width), 0) // rows
    column_of = lax.broadcasted_iota(jnp.int32, (width, width), 1) // rows

    def shard_at(index, carry):
        start = pl.multiple_of(order_ref[index] * width, width)
        counts = count_of(ids_ref[:, pl.ds(start, width)], order_ref[0] * rows, rows)
        tall = jnp.concatenate([counts] * QUAD, axis=0)
        blocks_ref[index] = jnp.where(row_of == column_of, tall, 0.0).astype(BF16)
        return carry

    lax.fori_loop(0, shards_of, shard_at, 0)
    done_ref[...] = jnp.zeros(done_ref.shape, done_ref.dtype)


def forward_body(
    quad_ref, table_ref, packed0_ref, packed1_ref, packed2_ref, packed3_ref, down_ref, up_ref,
    state_ref, part_ref, ids_ref, counts_ref,
):
    packed_refs = (packed0_ref, packed1_ref, packed2_ref, packed3_ref)
    samples = state_ref.shape[1]
    group = samples // QUAD
    rows = 64
    ids_ref[...] = ids_of(quad_ref, packed_refs, samples)

    def rows_at(index, carry):
        base = pl.multiple_of(index * rows, rows)
        counts_ref[pl.ds(base, rows), :] = count_of(ids_ref[...], base, rows).astype(BF16)
        return carry

    lax.fori_loop(0, counts_ref.shape[0] // rows, rows_at, 0)
    pooled = contract(counts_ref[...], table_ref[...], 0, 0).astype(BF16)
    state_ref[0] = pooled
    for step, packed_ref in enumerate(packed_refs):
        state_ref[1, step * group : (step + 1) * group, :] = packed_ref[:group, :]
    scaled = (state_ref[1].astype(F32) * pooled.astype(F32)).astype(BF16)
    rank_part = contract(pooled, down_ref[...], 1, 0).astype(BF16)
    back_part = contract(scaled, up_ref[...], 1, 1).astype(BF16)
    for step in range(QUAD):
        rows_of = place_of(quad_ref, step, group)
        part_ref[0, rows_of, :] = rank_part[step * group : (step + 1) * group]
        part_ref[1, rows_of, :] = back_part[step * group : (step + 1) * group]


def cross_body(
    quad_ref, ranks_ref, state_ref, down_ref, up_ref,
    parts_ref, back0_ref, back1_ref, back2_ref, back3_ref,
):
    group = state_ref.shape[1] // QUAD

    def in_steps(index):
        return jnp.concatenate(
            [ranks_ref[index, place_of(quad_ref, step, group), :] for step in range(QUAD)], axis=0
        )

    rank_act = in_steps(0)
    rank_grad = in_steps(1)
    pooled = state_ref[0]
    pooled_f = pooled.astype(F32)
    upstream = state_ref[1].astype(F32)
    scaled = (upstream * pooled_f).astype(BF16)
    parts_ref[0] = contract(rank_act, scaled, 0, 0).astype(BF16)
    parts_ref[1] = contract(pooled, rank_grad, 0, 0).astype(BF16)
    scale_map = contract(rank_act, up_ref[...], 1, 0)
    cross = (pooled_f * scale_map + pooled_f).astype(BF16)
    back = contract(rank_grad, down_ref[...], 1, 1)
    pooled_grad = (upstream * scale_map + upstream + back).astype(BF16)
    for step, one_ref in enumerate((back0_ref, back1_ref, back2_ref, back3_ref)):
        one_ref[0] = cross[step * group : (step + 1) * group]
        one_ref[1] = pooled_grad[step * group : (step + 1) * group]


def add_body(slices_ref, copies_ref):
    total = jnp.sum(slices_ref[...].astype(F32), axis=0).astype(BF16)
    for index in range(copies_ref.shape[0]):
        copies_ref[index] = total


def copy_body(value_ref, copies_ref):
    for index in range(copies_ref.shape[0]):
        copies_ref[index] = value_ref[...]


def arrange_body(quad_ref, back0_ref, back1_ref, back2_ref, back3_ref, cross_ref, pooled_grad_ref):
    embed = back0_ref.shape[2]
    for step, one_ref in enumerate((back0_ref, back1_ref, back2_ref, back3_ref)):
        cross_ref[:, place_of(quad_ref, step, embed)] = one_ref[0]
        pooled_grad_ref[lax.bitwise_xor(quad_ref[0], step)] = one_ref[1]


def table_body(order_ref, blocks_ref, grads_ref, out_ref):
    count, width, _ = blocks_ref.shape
    _, rows, embed = out_ref.shape
    first = pl.program_id(0) * count
    for index in range(count):
        grads = grads_ref[index * QUAD : (index + 1) * QUAD].reshape(width, embed)
        sums = contract(blocks_ref[index], grads, 1, 0).astype(BF16)
        start = order_ref[first + index] * QUAD
        for feature in range(QUAD):
            out_ref[start + feature] = sums[feature * rows : (feature + 1) * rows]


def sum_tables(order, blocks, grads):
    features, group, embed = grads.shape
    shards_of, width, _ = blocks.shape
    count = shards_of // 4
    out = (features, width // QUAD, embed)
    return pl.pallas_call(
        table_body,
        out_shape=shape_of(out),
        grid_spec=pltpu.PrefetchScalarGridSpec(
            num_scalar_prefetch=1,
            grid=(4,),
            in_specs=[
                pl.BlockSpec((count, width, width), lambda index, order: (index, 0, 0)),
                pl.BlockSpec((count * QUAD, group, embed), lambda index, order: (index, 0, 0)),
            ],
            out_specs=pl.BlockSpec(out, lambda index, order: (0, 0, 0)),
        ),
        compiler_params=pltpu.CompilerParams(vmem_limit_bytes=VMEM_LIMIT),
    )(order, blocks, grads)


def weights_body(sums_ref, down_ref, up_ref):
    width = sums_ref.shape[3]
    for quad in range(QUAD):
        span = slice(quad * width, (quad + 1) * width)
        up_ref[:, span] = sums_ref[quad, 0].astype(F32)
        down_ref[span, :] = sums_ref[quad, 1].astype(F32)


def shape_of(shape, dtype=BF16):
    return jax.ShapeDtypeStruct(shape, dtype)


def shards(bag_ids, tables, down_proj, up_proj, cotangent):
    dp_count, ways = lax.axis_size("dp"), lax.axis_size("mp")
    depth = dp_count // 2
    quads, lines, blocks = layout_of(dp_count, ways)
    pairs, members = len(lines[0]), len(blocks[0])
    place = lax.axis_index("dp")
    quad = (place // depth) * 2 + place % 2
    quad_at = quad.reshape(1)
    shard_index = lax.axis_index("mp")
    group, feature_count, bag_size = bag_ids.shape
    _, rows, embed = tables.shape
    rank = down_proj.shape[1]
    samples = QUAD * group

    def exchange(value, axis, groups=None):
        return lax.all_to_all(value, axis, 0, 0, axis_index_groups=groups, tiled=True)

    def swap(values):
        got = [values[0]]
        for step in range(1, QUAD):
            mask = (step // 2) * depth + step % 2
            pairs = [(index, index ^ mask) for index in range(dp_count)]
            got.append(lax.ppermute(values[step], "dp", pairs))
        return got

    def double(value, mask):
        other = lax.ppermute(value, "mp", [(index, index ^ mask) for index in range(ways)])
        return jnp.concatenate([value, other], axis=0), other

    with jax.named_scope("inputs"):
        table_parts = call_sliced(
            slice_body, shape_of((ways, rows, embed)), quad_at, (),
            ((tables.reshape(ways, QUAD, rows, embed), 1),), limit=5 * VMEM_LIMIT,
        )
        table = exchange(table_parts, "mp").reshape(ways * rows, embed)
        ids = jnp.transpose(bag_ids, (2, 1, 0)).reshape(bag_size, feature_count * group)
        packed_shape = shape_of((group + 2 * bag_size, embed))
        packed = swap(
            call(pack_body, (packed_shape,) * QUAD, quad_at, shard_index.reshape(1), ids, cotangent)
        )
        weights = ((down_proj, 0), (up_proj, 1))

    with jax.named_scope("counts"):
        steps = [ways >> (index + 1) for index in range(ways.bit_length() - 1)]
        order = [shard_index]
        for mask in steps:
            order = order + [index ^ mask for index in order]
        order = jnp.stack(order)
        row_blocks, done = call(
            block_body, (shape_of((ways, QUAD * rows, QUAD * group)), shape_of((8, 128), F32)), order, ids
        )

    with jax.named_scope("forward"):
        state, part = call_sliced(
            forward_body, (shape_of((2, samples, embed)), shape_of((2, samples, rank))),
            quad_at, (table, *packed), weights,
            (pltpu.VMEM((bag_size, samples), jnp.int32), pltpu.VMEM((ways * rows, samples), BF16)),
        )
    with jax.named_scope("ranks"):
        piece = 2 * samples // members
        pieces = exchange(part.reshape(members, piece, rank), ("dp", "mp"), blocks)
        copies = call(add_body, shape_of((members, piece, rank)), pieces, after=(done,))
        ranks = exchange(copies, ("dp", "mp"), blocks).reshape(2, samples, rank)

    with jax.named_scope("cross"):
        parts, *backs = call_sliced(
            cross_body, (shape_of((2, embed, rank)),) + (shape_of((2, group, embed)),) * QUAD,
            quad_at, (ranks, state), weights,
        )

    slab = (2 * embed // pairs, rank)
    with jax.named_scope("line_sums"):
        line_parts = exchange(parts.reshape((pairs,) + slab), "dp", lines)
        cross_out, grads = call(
            arrange_body, (shape_of((group, QUAD * embed)), shape_of((QUAD, group, embed))),
            quad_at, *swap(backs),
        )
        grads, arrived = double(grads, steps[0])
        copies = call(add_body, shape_of((pairs,) + slab), line_parts, after=(arrived,))
    with jax.named_scope("line_gather"):
        sums = exchange(copies, "dp", lines)
        for mask in steps[1:-1]:
            grads, arrived = double(grads, mask)
        quad_copies = call(copy_body, shape_of((QUAD, pairs) + slab), sums, after=(arrived,))
    with jax.named_scope("quad_gather"):
        every = exchange(quad_copies, "dp", quads).reshape(QUAD, 2, embed, rank)
        grads, _ = double(grads, steps[-1])
        table_grads = sum_tables(order, row_blocks, grads)[None]
        down_grad, up_grad = call(
            weights_body, (shape_of(down_proj.shape, F32), shape_of(up_proj.shape, F32)), every
        )
    return (cross_out, table_grads, down_grad, up_grad)


def solution(mesh):
    placed = (P("dp", None, None), P(None, "mp", None), P("mp", None), P(None, "mp"), P("dp", "mp"))
    return jax.shard_map(
        shards,
        mesh=mesh,
        in_specs=placed,
        out_specs=(P("dp", "mp"), P("dp", None, "mp", None), P("mp", None), P(None, "mp")),
        check_vma=False,
    )
```

```python
import math

import jax
import jax.numpy as jnp
from jax import lax
from jax.experimental import pallas as pl
from jax.experimental.pallas import tpu as pltpu
from jax.sharding import PartitionSpec as P

BF16 = jnp.bfloat16
F32 = jnp.float32
VMEM_LIMIT = 12 * 1024 * 1024

QUAD = 4
ID_BITS = 5


def layout_of(dp_count, mp_count):
    depth = dp_count // 2
    pairs = depth // 2

    def member(pair, quad):
        return (quad // 2) * depth + pair * 2 + quad % 2

    window = math.isqrt(pairs)
    quads = [[member(pair, quad) for quad in range(QUAD)] for pair in range(pairs)]
    near = [
        [member(start + index, quad) for index in range(window)]
        for quad in range(QUAD)
        for start in range(0, pairs, window)
    ]
    far = [
        [member(pair, quad) for pair in range(index, pairs, window)]
        for quad in range(QUAD)
        for index in range(window)
    ]
    blocks = [
        [member(pair, quad) * mp_count + index for index in range(mp_count) for quad in range(QUAD)]
        for pair in range(pairs)
    ]
    return quads, near, far, blocks


def call(body, out_shape, *operands, after=()):
    def run(*refs):
        body(*refs[: len(operands)], *refs[len(operands) + len(after) :])

    return pl.pallas_call(
        run,
        out_shape=out_shape,
        in_specs=[
            pl.BlockSpec(memory_space=pltpu.SMEM if operand.ndim == 1 else pltpu.VMEM)
            for operand in operands
        ]
        + [pl.BlockSpec(memory_space=pl.ANY)] * len(after),
        compiler_params=pltpu.CompilerParams(vmem_limit_bytes=VMEM_LIMIT),
    )(*operands, *after)


def call_sliced(body, out_shape, quad_at, operands, sliced, scratch=(), limit=VMEM_LIMIT):
    def whole(array):
        return pl.BlockSpec(array.shape, lambda index, quad: (0,) * len(array.shape))

    def part(array, dim):
        shape = list(array.shape)
        shape[dim] //= QUAD
        return pl.BlockSpec(
            tuple(shape),
            lambda index, quad: tuple(quad[0] if axis == dim else 0 for axis in range(len(shape))),
        )

    return pl.pallas_call(
        body,
        out_shape=out_shape,
        grid_spec=pltpu.PrefetchScalarGridSpec(
            num_scalar_prefetch=1,
            grid=(1,),
            in_specs=[whole(operand) for operand in operands] + [part(*pair) for pair in sliced],
            out_specs=jax.tree.map(whole, out_shape),
            scratch_shapes=scratch,
        ),
        compiler_params=pltpu.CompilerParams(vmem_limit_bytes=limit),
    )(quad_at, *operands, *(array for array, _ in sliced))


def contract(left, right, left_dim, right_dim):
    return lax.dot_general(
        left, right, (((left_dim,), (right_dim,)), ((), ())), preferred_element_type=F32
    )


def place_of(quad_ref, step, extent):
    return pl.ds(pl.multiple_of(lax.bitwise_xor(quad_ref[0], step) * extent, extent), extent)


def count_of(ids, base, rows):
    slots = lax.broadcasted_iota(jnp.int32, (rows, ids.shape[1]), 0) + base
    total = jnp.zeros(slots.shape, F32)
    for slot in range(ids.shape[0]):
        total = total + jnp.where(slots == ids[slot : slot + 1, :], 1.0, 0.0)
    return total


def slice_body(quad_ref, source_ref, slice_ref):
    slice_ref[...] = source_ref[:, 0]


def pack_body(quad_ref, shard_ref, ids_ref, grad_ref, *packed_refs):
    group, width = grad_ref.shape
    bag_size = ids_ref.shape[0]
    embed = width // QUAD
    span = QUAD * group
    own = ids_ref[:, pl.ds(pl.multiple_of(shard_ref[0] * span, span), span)]
    high = lax.shift_right_logical(own, ID_BITS).astype(F32).astype(BF16)
    low = lax.bitwise_and(own, (1 << ID_BITS) - 1).astype(F32).astype(BF16)
    for step, packed_ref in enumerate(packed_refs):
        packed_ref[:group, :] = grad_ref[:, place_of(quad_ref, step, embed)]
        packed_ref[group : group + bag_size, :] = high
        packed_ref[group + bag_size :, :] = low


def ids_of(quad_ref, packed_refs, columns):
    group = columns // QUAD
    bag_size = (packed_refs[0].shape[0] - group) // 2
    lanes = lax.broadcasted_iota(jnp.int32, (bag_size, columns), 1)
    ids = jnp.zeros((bag_size, columns), jnp.int32)
    for step, packed_ref in enumerate(packed_refs):
        high = packed_ref[group : group + bag_size, :].astype(F32)
        low = packed_ref[group + bag_size :, :].astype(F32)
        every = (high * (1 << ID_BITS) + low).astype(jnp.int32)
        turn = lax.bitwise_and(step - quad_ref[0], QUAD - 1) * group
        here = (lanes >= step * group) & (lanes < (step + 1) * group)
        ids = jnp.where(here, pltpu.roll(every, turn, 1), ids)
    return ids


def block_body(order_ref, ids_ref, blocks_ref, done_ref):
    shards_of, width, _ = blocks_ref.shape
    rows = width // QUAD
    row_of = lax.broadcasted_iota(jnp.int32, (width, width), 0) // rows
    column_of = lax.broadcasted_iota(jnp.int32, (width, width), 1) // rows

    def shard_at(index, carry):
        start = pl.multiple_of(order_ref[index] * width, width)
        counts = count_of(ids_ref[:, pl.ds(start, width)], order_ref[0] * rows, rows)
        tall = jnp.concatenate([counts] * QUAD, axis=0)
        blocks_ref[index] = jnp.where(row_of == column_of, tall, 0.0).astype(BF16)
        return carry

    lax.fori_loop(0, shards_of, shard_at, 0)
    done_ref[...] = jnp.zeros(done_ref.shape, done_ref.dtype)


def forward_body(
    quad_ref, table_ref, packed0_ref, packed1_ref, packed2_ref, packed3_ref, down_ref, up_ref,
    state_ref, part_ref, ids_ref, counts_ref,
):
    packed_refs = (packed0_ref, packed1_ref, packed2_ref, packed3_ref)
    samples = state_ref.shape[1]
    group = samples // QUAD
    rows = 64
    ids_ref[...] = ids_of(quad_ref, packed_refs, samples)

    def rows_at(index, carry):
        base = pl.multiple_of(index * rows, rows)
        counts_ref[pl.ds(base, rows), :] = count_of(ids_ref[...], base, rows).astype(BF16)
        return carry

    lax.fori_loop(0, counts_ref.shape[0] // rows, rows_at, 0)
    pooled = contract(counts_ref[...], table_ref[...], 0, 0).astype(BF16)
    state_ref[0] = pooled
    for step, packed_ref in enumerate(packed_refs):
        state_ref[1, step * group : (step + 1) * group, :] = packed_ref[:group, :]
    scaled = (state_ref[1].astype(F32) * pooled.astype(F32)).astype(BF16)
    rank_part = contract(pooled, down_ref[...], 1, 0).astype(BF16)
    back_part = contract(scaled, up_ref[...], 1, 1).astype(BF16)
    for step in range(QUAD):
        rows_of = place_of(quad_ref, step, group)
        part_ref[0, rows_of, :] = rank_part[step * group : (step + 1) * group]
        part_ref[1, rows_of, :] = back_part[step * group : (step + 1) * group]


def cross_body(
    quad_ref, ranks_ref, state_ref, down_ref, up_ref,
    parts_ref, back0_ref, back1_ref, back2_ref, back3_ref,
):
    group = state_ref.shape[1] // QUAD

    def in_steps(index):
        return jnp.concatenate(
            [ranks_ref[index, place_of(quad_ref, step, group), :] for step in range(QUAD)], axis=0
        )

    rank_act = in_steps(0)
    rank_grad = in_steps(1)
    pooled = state_ref[0]
    pooled_f = pooled.astype(F32)
    upstream = state_ref[1].astype(F32)
    scaled = (upstream * pooled_f).astype(BF16)
    parts_ref[0] = contract(rank_act, scaled, 0, 0).astype(BF16)
    parts_ref[1] = contract(pooled, rank_grad, 0, 0).astype(BF16)
    scale_map = contract(rank_act, up_ref[...], 1, 0)
    cross = (pooled_f * scale_map + pooled_f).astype(BF16)
    back = contract(rank_grad, down_ref[...], 1, 1)
    pooled_grad = (upstream * scale_map + upstream + back).astype(BF16)
    for step, one_ref in enumerate((back0_ref, back1_ref, back2_ref, back3_ref)):
        one_ref[0] = cross[step * group : (step + 1) * group]
        one_ref[1] = pooled_grad[step * group : (step + 1) * group]


def add_body(slices_ref, copies_ref):
    total = jnp.sum(slices_ref[...].astype(F32), axis=0).astype(BF16)
    for index in range(copies_ref.shape[0]):
        copies_ref[index] = total


def copy_body(value_ref, copies_ref):
    for index in range(copies_ref.shape[0]):
        copies_ref[index] = value_ref[...]


def arrange_body(quad_ref, back0_ref, back1_ref, back2_ref, back3_ref, cross_ref, pooled_grad_ref):
    embed = back0_ref.shape[2]
    for step, one_ref in enumerate((back0_ref, back1_ref, back2_ref, back3_ref)):
        cross_ref[:, place_of(quad_ref, step, embed)] = one_ref[0]
        pooled_grad_ref[lax.bitwise_xor(quad_ref[0], step)] = one_ref[1]


def table_body(order_ref, blocks_ref, grads_ref, out_ref):
    count, width, _ = blocks_ref.shape
    _, rows, embed = out_ref.shape
    first = pl.program_id(0) * count
    for index in range(count):
        grads = grads_ref[index * QUAD : (index + 1) * QUAD].reshape(width, embed)
        sums = contract(blocks_ref[index], grads, 1, 0).astype(BF16)
        start = order_ref[first + index] * QUAD
        for feature in range(QUAD):
            out_ref[start + feature] = sums[feature * rows : (feature + 1) * rows]


def sum_tables(order, blocks, grads):
    features, group, embed = grads.shape
    shards_of, width, _ = blocks.shape
    count = shards_of // 4
    out = (features, width // QUAD, embed)
    return pl.pallas_call(
        table_body,
        out_shape=shape_of(out),
        grid_spec=pltpu.PrefetchScalarGridSpec(
            num_scalar_prefetch=1,
            grid=(4,),
            in_specs=[
                pl.BlockSpec((count, width, width), lambda index, order: (index, 0, 0)),
                pl.BlockSpec((count * QUAD, group, embed), lambda index, order: (index, 0, 0)),
            ],
            out_specs=pl.BlockSpec(out, lambda index, order: (0, 0, 0)),
        ),
        compiler_params=pltpu.CompilerParams(vmem_limit_bytes=VMEM_LIMIT),
    )(order, blocks, grads)


def weights_body(sums_ref, down_ref, up_ref):
    width = sums_ref.shape[3]
    for quad in range(QUAD):
        span = slice(quad * width, (quad + 1) * width)
        up_ref[:, span] = sums_ref[quad, 0].astype(F32)
        down_ref[span, :] = sums_ref[quad, 1].astype(F32)


def shape_of(shape, dtype=BF16):
    return jax.ShapeDtypeStruct(shape, dtype)


def shards(bag_ids, tables, down_proj, up_proj, cotangent):
    dp_count, ways = lax.axis_size("dp"), lax.axis_size("mp")
    depth = dp_count // 2
    quads, near, far, blocks = layout_of(dp_count, ways)
    window, windows, members = len(near[0]), len(far[0]), len(blocks[0])
    place = lax.axis_index("dp")
    quad = (place // depth) * 2 + place % 2
    quad_at = quad.reshape(1)
    shard_index = lax.axis_index("mp")
    group, feature_count, bag_size = bag_ids.shape
    _, rows, embed = tables.shape
    rank = down_proj.shape[1]
    samples = QUAD * group

    def exchange(value, axis, groups=None):
        return lax.all_to_all(value, axis, 0, 0, axis_index_groups=groups, tiled=True)

    def swap(values):
        got = [values[0]]
        for step in range(1, QUAD):
            mask = (step // 2) * depth + step % 2
            pairs = [(index, index ^ mask) for index in range(dp_count)]
            got.append(lax.ppermute(values[step], "dp", pairs))
        return got

    def double(value, mask):
        other = lax.ppermute(value, "mp", [(index, index ^ mask) for index in range(ways)])
        return jnp.concatenate([value, other], axis=0), other

    with jax.named_scope("inputs"):
        table_parts = call_sliced(
            slice_body, shape_of((ways, rows, embed)), quad_at, (),
            ((tables.reshape(ways, QUAD, rows, embed), 1),), limit=5 * VMEM_LIMIT,
        )
        table = exchange(table_parts, "mp").reshape(ways * rows, embed)
        ids = jnp.transpose(bag_ids, (2, 1, 0)).reshape(bag_size, feature_count * group)
        packed_shape = shape_of((group + 2 * bag_size, embed))
        packed = swap(
            call(pack_body, (packed_shape,) * QUAD, quad_at, shard_index.reshape(1), ids, cotangent)
        )
        weights = ((down_proj, 0), (up_proj, 1))

    with jax.named_scope("counts"):
        steps = [ways >> (index + 1) for index in range(ways.bit_length() - 1)]
        order = [shard_index]
        for mask in steps:
            order = order + [index ^ mask for index in order]
        order = jnp.stack(order)
        row_blocks, done = call(
            block_body, (shape_of((ways, QUAD * rows, QUAD * group)), shape_of((8, 128), F32)), order, ids
        )

    with jax.named_scope("forward"):
        state, part = call_sliced(
            forward_body, (shape_of((2, samples, embed)), shape_of((2, samples, rank))),
            quad_at, (table, *packed), weights,
            (pltpu.VMEM((bag_size, samples), jnp.int32), pltpu.VMEM((ways * rows, samples), BF16)),
        )
    with jax.named_scope("ranks"):
        piece = 2 * samples // members
        pieces = exchange(part.reshape(members, piece, rank), ("dp", "mp"), blocks)
        copies = call(add_body, shape_of((members, piece, rank)), pieces, after=(done,))
        ranks = exchange(copies, ("dp", "mp"), blocks).reshape(2, samples, rank)

    with jax.named_scope("cross"):
        parts, *backs = call_sliced(
            cross_body, (shape_of((2, embed, rank)),) + (shape_of((2, group, embed)),) * QUAD,
            quad_at, (ranks, state), weights,
        )

    slab = (2 * embed // window, rank)
    with jax.named_scope("near_sums"):
        near_parts = exchange(parts.reshape((window,) + slab), "dp", near)
        cross_out, grads = call(
            arrange_body, (shape_of((group, QUAD * embed)), shape_of((QUAD, group, embed))),
            quad_at, *swap(backs),
        )
        near_copies = call(add_body, shape_of((windows,) + slab), near_parts, after=(grads,))
    with jax.named_scope("far_sums"):
        far_parts = exchange(near_copies, "dp", far)
        for mask in steps[:-1]:
            grads, arrived = double(grads, mask)
        far_copies = call(add_body, shape_of((window,) + slab), far_parts, after=(arrived,))
    with jax.named_scope("near_gather"):
        sums = exchange(far_copies, "dp", near)
        grads, arrived = double(grads, steps[-1])
        quad_copies = call(
            copy_body, shape_of((QUAD, window) + slab), sums, after=(arrived,)
        )
    with jax.named_scope("quad_gather"):
        every = exchange(quad_copies, "dp", quads).reshape(QUAD, 2, embed, rank)
        table_grads = sum_tables(order, row_blocks, grads)[None]
        down_grad, up_grad = call(
            weights_body, (shape_of(down_proj.shape, F32), shape_of(up_proj.shape, F32)), every
        )
    return (cross_out, table_grads, down_grad, up_grad)


def solution(mesh):
    placed = (P("dp", None, None), P(None, "mp", None), P("mp", None), P(None, "mp"), P("dp", "mp"))
    return jax.shard_map(
        shards,
        mesh=mesh,
        in_specs=placed,
        out_specs=(P("dp", "mp"), P("dp", None, "mp", None), P("mp", None), P(None, "mp")),
        check_vma=False,
    )
```

```python
import math

import jax
import jax.numpy as jnp
from jax import lax
from jax.experimental import pallas as pl
from jax.experimental.pallas import tpu as pltpu
from jax.sharding import PartitionSpec as P

BF16 = jnp.bfloat16
F32 = jnp.float32
VMEM_LIMIT = 12 * 1024 * 1024

QUAD = 4
ID_BITS = 5


def layout_of(dp_count, mp_count):
    depth = dp_count // 2
    pairs = depth // 2

    def member(pair, quad):
        return (quad // 2) * depth + pair * 2 + quad % 2

    window = math.isqrt(pairs)
    quads = [[member(pair, quad) for quad in range(QUAD)] for pair in range(pairs)]
    near = [
        [member(start + index, quad) for index in range(window)]
        for quad in range(QUAD)
        for start in range(0, pairs, window)
    ]
    far = [
        [member(pair, quad) for pair in range(index, pairs, window)]
        for quad in range(QUAD)
        for index in range(window)
    ]
    blocks = [
        [member(pair, quad) * mp_count + index for index in range(mp_count) for quad in range(QUAD)]
        for pair in range(pairs)
    ]
    return quads, near, far, blocks


def call(body, out_shape, *operands, after=()):
    def run(*refs):
        body(*refs[: len(operands)], *refs[len(operands) + len(after) :])

    return pl.pallas_call(
        run,
        out_shape=out_shape,
        in_specs=[
            pl.BlockSpec(memory_space=pltpu.SMEM if operand.ndim == 1 else pltpu.VMEM)
            for operand in operands
        ]
        + [pl.BlockSpec(memory_space=pl.ANY)] * len(after),
        compiler_params=pltpu.CompilerParams(vmem_limit_bytes=VMEM_LIMIT),
    )(*operands, *after)


def call_sliced(body, out_shape, quad_at, operands, sliced, scratch=(), limit=VMEM_LIMIT):
    def whole(array):
        return pl.BlockSpec(array.shape, lambda index, quad: (0,) * len(array.shape))

    def part(array, dim):
        shape = list(array.shape)
        shape[dim] //= QUAD
        return pl.BlockSpec(
            tuple(shape),
            lambda index, quad: tuple(quad[0] if axis == dim else 0 for axis in range(len(shape))),
        )

    return pl.pallas_call(
        body,
        out_shape=out_shape,
        grid_spec=pltpu.PrefetchScalarGridSpec(
            num_scalar_prefetch=1,
            grid=(1,),
            in_specs=[whole(operand) for operand in operands] + [part(*pair) for pair in sliced],
            out_specs=jax.tree.map(whole, out_shape),
            scratch_shapes=scratch,
        ),
        compiler_params=pltpu.CompilerParams(vmem_limit_bytes=limit),
    )(quad_at, *operands, *(array for array, _ in sliced))


def contract(left, right, left_dim, right_dim):
    return lax.dot_general(
        left, right, (((left_dim,), (right_dim,)), ((), ())), preferred_element_type=F32
    )


def place_of(quad_ref, step, extent):
    return pl.ds(pl.multiple_of(lax.bitwise_xor(quad_ref[0], step) * extent, extent), extent)


def count_of(ids, base, rows):
    slots = lax.broadcasted_iota(jnp.int32, (rows, ids.shape[1]), 0) + base
    total = jnp.zeros(slots.shape, F32)
    for slot in range(ids.shape[0]):
        total = total + jnp.where(slots == ids[slot : slot + 1, :], 1.0, 0.0)
    return total


def slice_body(quad_ref, source_ref, slice_ref):
    slice_ref[...] = source_ref[:, 0]


def pack_body(quad_ref, shard_ref, ids_ref, grad_ref, *packed_refs):
    group, width = grad_ref.shape
    bag_size = ids_ref.shape[0]
    embed = width // QUAD
    span = QUAD * group
    own = ids_ref[:, pl.ds(pl.multiple_of(shard_ref[0] * span, span), span)]
    high = lax.shift_right_logical(own, ID_BITS).astype(F32).astype(BF16)
    low = lax.bitwise_and(own, (1 << ID_BITS) - 1).astype(F32).astype(BF16)
    for step, packed_ref in enumerate(packed_refs):
        packed_ref[:group, :] = grad_ref[:, place_of(quad_ref, step, embed)]
        packed_ref[group : group + bag_size, :] = high
        packed_ref[group + bag_size :, :] = low


def ids_of(quad_ref, packed_refs, columns):
    group = columns // QUAD
    bag_size = (packed_refs[0].shape[0] - group) // 2
    lanes = lax.broadcasted_iota(jnp.int32, (bag_size, columns), 1)
    ids = jnp.zeros((bag_size, columns), jnp.int32)
    for step, packed_ref in enumerate(packed_refs):
        high = packed_ref[group : group + bag_size, :].astype(F32)
        low = packed_ref[group + bag_size :, :].astype(F32)
        every = (high * (1 << ID_BITS) + low).astype(jnp.int32)
        turn = lax.bitwise_and(step - quad_ref[0], QUAD - 1) * group
        here = (lanes >= step * group) & (lanes < (step + 1) * group)
        ids = jnp.where(here, pltpu.roll(every, turn, 1), ids)
    return ids


def block_body(order_ref, ids_ref, blocks_ref, done_ref):
    shards_of, width, _ = blocks_ref.shape
    rows = width // QUAD
    row_of = lax.broadcasted_iota(jnp.int32, (width, width), 0) // rows
    column_of = lax.broadcasted_iota(jnp.int32, (width, width), 1) // rows

    def shard_at(index, carry):
        start = pl.multiple_of(order_ref[index] * width, width)
        counts = count_of(ids_ref[:, pl.ds(start, width)], order_ref[0] * rows, rows)
        tall = jnp.concatenate([counts] * QUAD, axis=0)
        blocks_ref[index] = jnp.where(row_of == column_of, tall, 0.0).astype(BF16)
        return carry

    lax.fori_loop(0, shards_of, shard_at, 0)
    done_ref[...] = jnp.zeros(done_ref.shape, done_ref.dtype)


def forward_body(
    quad_ref, table_ref, packed0_ref, packed1_ref, packed2_ref, packed3_ref, down_ref, up_ref,
    state_ref, part_ref, ids_ref, counts_ref,
):
    packed_refs = (packed0_ref, packed1_ref, packed2_ref, packed3_ref)
    samples = state_ref.shape[1]
    group = samples // QUAD
    rows = 64
    ids_ref[...] = ids_of(quad_ref, packed_refs, samples)

    def rows_at(index, carry):
        base = pl.multiple_of(index * rows, rows)
        counts_ref[pl.ds(base, rows), :] = count_of(ids_ref[...], base, rows).astype(BF16)
        return carry

    lax.fori_loop(0, counts_ref.shape[0] // rows, rows_at, 0)
    pooled = contract(counts_ref[...], table_ref[...], 0, 0).astype(BF16)
    state_ref[0] = pooled
    for step, packed_ref in enumerate(packed_refs):
        state_ref[1, step * group : (step + 1) * group, :] = packed_ref[:group, :]
    scaled = (state_ref[1].astype(F32) * pooled.astype(F32)).astype(BF16)
    rank_part = contract(pooled, down_ref[...], 1, 0).astype(BF16)
    back_part = contract(scaled, up_ref[...], 1, 1).astype(BF16)
    for step in range(QUAD):
        rows_of = place_of(quad_ref, step, group)
        part_ref[0, rows_of, :] = rank_part[step * group : (step + 1) * group]
        part_ref[1, rows_of, :] = back_part[step * group : (step + 1) * group]


def cross_body(
    quad_ref, ranks_ref, state_ref, down_ref, up_ref,
    parts_ref, back0_ref, back1_ref, back2_ref, back3_ref,
):
    group = state_ref.shape[1] // QUAD

    def in_steps(index):
        return jnp.concatenate(
            [ranks_ref[index, place_of(quad_ref, step, group), :] for step in range(QUAD)], axis=0
        )

    rank_act = in_steps(0)
    rank_grad = in_steps(1)
    pooled = state_ref[0]
    pooled_f = pooled.astype(F32)
    upstream = state_ref[1].astype(F32)
    scaled = (upstream * pooled_f).astype(BF16)
    parts_ref[0] = contract(rank_act, scaled, 0, 0).astype(BF16)
    parts_ref[1] = contract(pooled, rank_grad, 0, 0).astype(BF16)
    scale_map = contract(rank_act, up_ref[...], 1, 0)
    cross = (pooled_f * scale_map + pooled_f).astype(BF16)
    back = contract(rank_grad, down_ref[...], 1, 1)
    pooled_grad = (upstream * scale_map + upstream + back).astype(BF16)
    for step, one_ref in enumerate((back0_ref, back1_ref, back2_ref, back3_ref)):
        one_ref[0] = cross[step * group : (step + 1) * group]
        one_ref[1] = pooled_grad[step * group : (step + 1) * group]


def add_body(slices_ref, copies_ref):
    total = jnp.sum(slices_ref[...].astype(F32), axis=0).astype(BF16)
    for index in range(copies_ref.shape[0]):
        copies_ref[index] = total


def copy_body(value_ref, copies_ref):
    for index in range(copies_ref.shape[0]):
        copies_ref[index] = value_ref[...]


def arrange_body(quad_ref, back0_ref, back1_ref, back2_ref, back3_ref, cross_ref, pooled_grad_ref):
    embed = back0_ref.shape[2]
    for step, one_ref in enumerate((back0_ref, back1_ref, back2_ref, back3_ref)):
        cross_ref[:, place_of(quad_ref, step, embed)] = one_ref[0]
        pooled_grad_ref[lax.bitwise_xor(quad_ref[0], step)] = one_ref[1]


def table_body(order_ref, blocks_ref, grads_ref, out_ref):
    count, width, _ = blocks_ref.shape
    _, rows, embed = out_ref.shape
    first = pl.program_id(0) * count
    for index in range(count):
        grads = grads_ref[index * QUAD : (index + 1) * QUAD].reshape(width, embed)
        sums = contract(blocks_ref[index], grads, 1, 0).astype(BF16)
        start = order_ref[first + index] * QUAD
        for feature in range(QUAD):
            out_ref[start + feature] = sums[feature * rows : (feature + 1) * rows]


def sum_tables(order, blocks, grads):
    features, group, embed = grads.shape
    shards_of, width, _ = blocks.shape
    count = shards_of // 4
    out = (features, width // QUAD, embed)
    return pl.pallas_call(
        table_body,
        out_shape=shape_of(out),
        grid_spec=pltpu.PrefetchScalarGridSpec(
            num_scalar_prefetch=1,
            grid=(4,),
            in_specs=[
                pl.BlockSpec((count, width, width), lambda index, order: (index, 0, 0)),
                pl.BlockSpec((count * QUAD, group, embed), lambda index, order: (index, 0, 0)),
            ],
            out_specs=pl.BlockSpec(out, lambda index, order: (0, 0, 0)),
        ),
        compiler_params=pltpu.CompilerParams(vmem_limit_bytes=VMEM_LIMIT),
    )(order, blocks, grads)


def weights_body(sums_ref, down_ref, up_ref):
    width = sums_ref.shape[3]
    for quad in range(QUAD):
        span = slice(quad * width, (quad + 1) * width)
        up_ref[:, span] = sums_ref[quad, 0].astype(F32)
        down_ref[span, :] = sums_ref[quad, 1].astype(F32)


def shape_of(shape, dtype=BF16):
    return jax.ShapeDtypeStruct(shape, dtype)


def shards(bag_ids, tables, down_proj, up_proj, cotangent):
    dp_count, ways = lax.axis_size("dp"), lax.axis_size("mp")
    depth = dp_count // 2
    quads, near, far, blocks = layout_of(dp_count, ways)
    window, windows, members = len(near[0]), len(far[0]), len(blocks[0])
    place = lax.axis_index("dp")
    quad = (place // depth) * 2 + place % 2
    quad_at = quad.reshape(1)
    shard_index = lax.axis_index("mp")
    group, feature_count, bag_size = bag_ids.shape
    _, rows, embed = tables.shape
    rank = down_proj.shape[1]
    samples = QUAD * group

    def exchange(value, axis, groups=None):
        return lax.all_to_all(value, axis, 0, 0, axis_index_groups=groups, tiled=True)

    def swap(values):
        got = [values[0]]
        for step in range(1, QUAD):
            mask = (step // 2) * depth + step % 2
            pairs = [(index, index ^ mask) for index in range(dp_count)]
            got.append(lax.ppermute(values[step], "dp", pairs))
        return got

    def other(value, mask):
        return lax.ppermute(value, "mp", [(index, index ^ mask) for index in range(ways)])

    def double(value, mask):
        arrived = other(value, mask)
        return jnp.concatenate([value, arrived], axis=0), arrived

    with jax.named_scope("inputs"):
        table_parts = call_sliced(
            slice_body, shape_of((ways, rows, embed)), quad_at, (),
            ((tables.reshape(ways, QUAD, rows, embed), 1),), limit=5 * VMEM_LIMIT,
        )
        table = exchange(table_parts, "mp").reshape(ways * rows, embed)
        ids = jnp.transpose(bag_ids, (2, 1, 0)).reshape(bag_size, feature_count * group)
        packed_shape = shape_of((group + 2 * bag_size, embed))
        packed = swap(
            call(pack_body, (packed_shape,) * QUAD, quad_at, shard_index.reshape(1), ids, cotangent)
        )
        weights = ((down_proj, 0), (up_proj, 1))

    with jax.named_scope("counts"):
        steps = [ways >> (index + 1) for index in range(ways.bit_length() - 1)]
        order = [shard_index]
        for mask in steps:
            order = order + [index ^ mask for index in order]
        order = jnp.stack(order)
        row_blocks, done = call(
            block_body, (shape_of((ways, QUAD * rows, QUAD * group)), shape_of((8, 128), F32)), order, ids
        )

    with jax.named_scope("forward"):
        state, part = call_sliced(
            forward_body, (shape_of((2, samples, embed)), shape_of((2, samples, rank))),
            quad_at, (table, *packed), weights,
            (pltpu.VMEM((bag_size, samples), jnp.int32), pltpu.VMEM((ways * rows, samples), BF16)),
        )
    with jax.named_scope("ranks"):
        piece = 2 * samples // members
        pieces = exchange(part.reshape(members, piece, rank), ("dp", "mp"), blocks)
        copies = call(add_body, shape_of((members, piece, rank)), pieces, after=(done,))
        ranks = exchange(copies, ("dp", "mp"), blocks).reshape(2, samples, rank)

    with jax.named_scope("cross"):
        parts, *backs = call_sliced(
            cross_body, (shape_of((2, embed, rank)),) + (shape_of((2, group, embed)),) * QUAD,
            quad_at, (ranks, state), weights,
        )

    slab = (2 * embed // window, rank)
    with jax.named_scope("near_sums"):
        near_parts = exchange(parts.reshape((window,) + slab), "dp", near)
        cross_out, grads = call(
            arrange_body, (shape_of((group, QUAD * embed)), shape_of((QUAD, group, embed))),
            quad_at, *swap(backs),
        )
        near_copies = call(add_body, shape_of((windows,) + slab), near_parts, after=(grads,))
    with jax.named_scope("far_sums"):
        far_parts = exchange(near_copies, "dp", far)
        first, second, third, last = steps
        masks = (first, second, first ^ second)
        grads = jnp.concatenate([grads] + [other(grads, mask) for mask in masks], axis=0)
        grads, arrived = double(grads, third)
        far_copies = call(add_body, shape_of((window,) + slab), far_parts, after=(arrived,))
    with jax.named_scope("near_gather"):
        sums = exchange(far_copies, "dp", near)
        grads, arrived = double(grads, last)
        quad_copies = call(
            copy_body, shape_of((QUAD, window) + slab), sums, after=(arrived,)
        )
    with jax.named_scope("quad_gather"):
        every = exchange(quad_copies, "dp", quads).reshape(QUAD, 2, embed, rank)
        table_grads = sum_tables(order, row_blocks, grads)[None]
        down_grad, up_grad = call(
            weights_body, (shape_of(down_proj.shape, F32), shape_of(up_proj.shape, F32)), every
        )
    return (cross_out, table_grads, down_grad, up_grad)


def solution(mesh):
    placed = (P("dp", None, None), P(None, "mp", None), P("mp", None), P(None, "mp"), P("dp", "mp"))
    return jax.shard_map(
        shards,
        mesh=mesh,
        in_specs=placed,
        out_specs=(P("dp", "mp"), P("dp", None, "mp", None), P("mp", None), P(None, "mp")),
        check_vma=False,
    )
```
